256 devices in a mesh: kern: 16 (over z_lo, x, core), slab: 16 (over y, z_hi).
Axes of the slice: x: 4, y: 4, z: 8 (z_hi: 4, z_lo: 2; z = z_hi * 2 + z_lo), core: 2. Of those that a mesh axis runs over, the one named last changes fastest.
Arguments:
- mask_params: float32 [2048, 2048], P('slab', 'kern'), may hold values from -6 to 6
- target_bits: int32 [2048, 2048], P('slab'), may hold values 0 or 1
- kernels: float32 [16, 2, 512, 512], P('kern', None, None, 'slab'), may hold values from -19.091883 to 19.091883
- weights: float32 [16], P('kern'), may hold values from 0.1 to 0.5
- dose_factors: float32 [2], replicated, may hold values from 0.25 to 1.75
Outputs:
- new_params: float32 [2048, 2048], P('slab', 'kern')
- resist_image: float32 [2, 2, 2048, 2048], P(None, None, 'slab', 'kern')
The draws below stay inside these ranges and needn't reach their ends.
All inputs are finite; a program needn't handle non-finite values. No bound on the sum of `target_bits` on one device may be relied on, other than what follows from the above.
Results may differ from the reference program's by a relative error of at most 0.035.
Values may be sent and summed in bfloat16 or wider, within the bound.
A program may use at most 128 MiB of HBM per device.

```python
import math
import jax
import jax.numpy as jnp
from jax import lax

N = 2048
F = 512
FOCI = 2
DOSES = 2
STEPS = 2
KERNELS = 16


def with_ends(result, stream_key, smallest, top_value):
    dims = result.shape
    spot = [jax.random.randint(jax.random.fold_in(stream_key, axis), (), 0, dims[axis]) for axis in range(len(dims))]
    result = result.at[tuple(spot)].set(smallest)
    longest = dims.index(max(dims))
    spot[longest] = (spot[longest] + 1) % dims[longest]
    return result.at[tuple(spot)].set(top_value)


def level_of(own_key, shape, pieces, smallest, high):
    def one(axis_at, parts):
        draws = jax.random.uniform(jax.random.fold_in(jax.random.fold_in(own_key, 6), axis_at), (parts,), jnp.float32, smallest / len(pieces), high / len(pieces))
        return jnp.repeat(jnp.exp(draws), shape[axis_at] // parts).reshape((-1,) + (1,) * (len(shape) - axis_at - 1))

    loudness = one(*pieces[0])
    for cut in pieces[1:]:
        loudness = loudness * one(*cut)
    return loudness


def centred(key, extent, deviation, limit, shards=(), kind=jnp.bfloat16):
    loudness = level_of(key, extent, shards, -0.22, 0.18) if shards else 1.0
    result = jax.random.normal(key, extent, jnp.float32) * deviation * loudness
    return jnp.minimum(jnp.maximum(result, -limit), limit).astype(kind)


def setup_inputs(seed: int = 0) -> dict:
    keys = jax.random.split(jax.random.key(seed), 6)
    return {
        "mask_params": centred(keys[0], (N, N), 1.0, 6.0, ((0, 16), (1, 16)), jnp.float32),
        "target_bits": with_ends((jax.random.randint(keys[1], (N, N), 0, 2) < 1).astype(jnp.int32), jax.random.fold_in(keys[1], 1), 0, 1),
        "kernels": centred(keys[2], (KERNELS, 2, F, F), (2.25 * (N // F) * (KERNELS // FOCI) ** -0.5), 19.091883, ((0, 16), (3, 16)), jnp.float32),
        "weights": jnp.clip(jnp.exp(math.log(0.5) - 1.609438 * jax.random.uniform(keys[3], (KERNELS,), jnp.float32) ** level_of(keys[3], (KERNELS,), ((0, 16),), -0.2, 0.2)), 0.1, 0.5),
        "dose_factors": jnp.clip(1.0 + 0.15 * jax.random.normal(keys[4], (DOSES,), jnp.float32), 0.25, 1.75),
    }


steepness = 3.0
threshold = 1.0
step_rate = 0.4

def times_transposed(left, right):
    return lax.dot_general(left, right, (((1,), (1,)), ((), ())), preferred_element_type=jnp.float32)

def transposed_times(left, right):
    return lax.dot_general(left, right, (((0,), (0,)), ((), ())), preferred_element_type=jnp.float32)

def plain_product(left, right):
    return jnp.dot(left, right, preferred_element_type=jnp.float32)

def tables():
    freqs = jnp.arange(F, dtype=jnp.int32) - F // 2
    pixels = jnp.arange(N, dtype=jnp.int32)
    phases = freqs[:, None] * pixels[None, :] % N
    angles = phases.astype(jnp.float32) * (2.0 * math.pi / N)
    scale = 1.0 / math.sqrt(N)
    return ((jnp.cos(angles) * scale).astype(jnp.bfloat16), (jnp.sin(angles) * scale).astype(jnp.bfloat16))

def resist(intensity, dose_factors, target_float):
    dose_grid = dose_factors[None, :, None, None]
    printed = jax.nn.sigmoid(steepness * (dose_grid * intensity[:, None] - threshold))
    errors = (printed - target_float) * printed * (1.0 - printed) * steepness * dose_grid
    return (printed, lax.optimization_barrier(jnp.sum(errors, axis=1)))

def reference(mask_params, target_bits, kernels, weights, dose_factors):
    cosine_table, sine_table = tables()
    stacked_table = jnp.concatenate([cosine_table, sine_table], axis=0)
    target_float = target_bits.astype(jnp.float32)
    foci_ids = jnp.arange(FOCI, dtype=jnp.int32)
    focus_index = jnp.arange(KERNELS, dtype=jnp.int32) % FOCI
    params = mask_params
    printed = None
    for iteration in range(STEPS):
        mask_values = jnp.tanh(params)
        mask_low = mask_values.astype(jnp.bfloat16)
        column_spec = times_transposed(mask_low, stacked_table)
        spec_in_real = column_spec[:, :F].astype(jnp.bfloat16)
        spec_in_imag = (-column_spec[:, F:]).astype(jnp.bfloat16)
        spec_real = plain_product(cosine_table, spec_in_real) + plain_product(sine_table, spec_in_imag)
        spec_imag = plain_product(cosine_table, spec_in_imag) - plain_product(sine_table, spec_in_real)

        def make_field(kernel_pair):
            filt_real = (kernel_pair[0] * spec_real - kernel_pair[1] * spec_imag).astype(jnp.bfloat16)
            filt_imag = (kernel_pair[0] * spec_imag + kernel_pair[1] * spec_real).astype(jnp.bfloat16)
            inv_real = (transposed_times(cosine_table, filt_real) - transposed_times(sine_table, filt_imag)).astype(jnp.bfloat16)
            inv_imag = (transposed_times(cosine_table, filt_imag) + transposed_times(sine_table, filt_real)).astype(jnp.bfloat16)
            field_real = plain_product(inv_real, cosine_table) - plain_product(inv_imag, sine_table)
            field_imag = plain_product(inv_real, sine_table) + plain_product(inv_imag, cosine_table)
            return (field_real, field_imag)

        def add_light(total, inputs):
            kernel_pair, kernel_weight, kernel_focus = inputs
            field_real, field_imag = make_field(kernel_pair)
            selector = (foci_ids == kernel_focus).astype(jnp.float32)
            power = kernel_weight * (field_real * field_real + field_imag * field_imag)
            return (total + selector[:, None, None] * power[None], None)
        intensity, unused = lax.scan(add_light, jnp.zeros((FOCI, N, N), jnp.float32), (kernels, weights, focus_index))
        printed, sens = resist(intensity, dose_factors, target_float)

        def add_grad(total, inputs):
            kernel_pair, kernel_weight, kernel_focus = inputs
            field_real, field_imag = make_field(kernel_pair)
            selector = (foci_ids == kernel_focus).astype(jnp.float32)
            kernel_sens = lax.optimization_barrier(jnp.sum(selector[:, None, None] * sens, axis=0))
            cot_real = (2.0 * kernel_weight * kernel_sens * field_real).astype(jnp.bfloat16)
            cot_imag = (2.0 * kernel_weight * kernel_sens * field_imag).astype(jnp.bfloat16)
            back_real = (times_transposed(cot_real, cosine_table) + times_transposed(cot_imag, sine_table)).astype(jnp.bfloat16)
            back_imag = (times_transposed(cot_imag, cosine_table) - times_transposed(cot_real, sine_table)).astype(jnp.bfloat16)
            grad_real = plain_product(cosine_table, back_real) + plain_product(sine_table, back_imag)
            grad_imag = plain_product(cosine_table, back_imag) - plain_product(sine_table, back_real)
            dspec_real = (kernel_pair[0] * grad_real + kernel_pair[1] * grad_imag).astype(jnp.bfloat16)
            dspec_imag = (kernel_pair[0] * grad_imag - kernel_pair[1] * grad_real).astype(jnp.bfloat16)
            adj_real = (transposed_times(cosine_table, dspec_real) - transposed_times(sine_table, dspec_imag)).astype(jnp.bfloat16)
            adj_imag = (transposed_times(sine_table, dspec_real) + transposed_times(cosine_table, dspec_imag)).astype(jnp.bfloat16)
            return (total + plain_product(adj_real, cosine_table) - plain_product(adj_imag, sine_table), None)
        mask_grad, unused = lax.scan(add_grad, jnp.zeros((N, N), jnp.float32), (kernels, weights, focus_index))
        params = params - step_rate * mask_grad * (1.0 - mask_values * mask_values)
    return (params, printed)
```

```python
import math

import jax
import jax.numpy as jnp
import ml_dtypes
import numpy as np
from jax import lax
from jax.experimental import pallas as pl
from jax.experimental.pallas import tpu as pltpu
from jax.sharding import PartitionSpec as P

N = 2048
F = 512
STEPS = 2
HALF = N // 2
EVEN = F // 2
SLABS = 16
KERNS = 16
MATES = 8

steepness = 3.0
threshold = 1.0
step_rate = 0.4
MESH = pl.DeviceIdType.MESH


def tables():
    index = np.concatenate([np.arange(0, F, 2), np.arange(1, F, 2)])
    pixels = np.arange(HALF)

    def pair(index, pixels):
        phases = ((index[:, None] - F // 2) * pixels[None, :]) % N
        angles = phases * (2.0 * math.pi / N)
        scale = 1.0 / math.sqrt(N)
        return np.cos(angles) * scale, np.sin(angles) * scale

    cos, sin = pair(index, pixels)
    to_pixels = np.concatenate([cos, sin], 1)
    from_pixels = np.concatenate([cos[:EVEN].T, sin[:EVEN].T, cos[EVEN:].T, sin[EVEN:].T], 1)
    k, s, i = np.meshgrid(np.arange(16), np.arange(8), np.arange(8), indexing="ij")
    owned = (s * 128 + k * 8 + i).reshape(-1)
    to_owned = np.concatenate([cos[:, owned], sin[:, owned]], 1)
    c, s = cos.reshape(2, EVEN, HALF)[:, :, owned], sin.reshape(2, EVEN, HALF)[:, :, owned]
    both = np.concatenate([c, s], 1).reshape(2, 2 * EVEN, 16, 64)
    from_owned = both.transpose(2, 0, 3, 1).reshape(N, 2 * EVEN)
    c, s = cos.reshape(2, 16, 16, HALF), sin.reshape(2, 16, 16, HALF)
    mixed = np.stack([c, -s]).transpose(2, 0, 1, 3, 4).reshape(2 * F, HALF)
    cast = lambda table: np.ascontiguousarray(table).astype(np.float32).astype(ml_dtypes.bfloat16)
    return [cast(t) for t in (mixed.T, from_owned, to_pixels, from_pixels, to_owned, mixed)]


def dot(left, right):
    return jnp.dot(left, right, preferred_element_type=jnp.float32)


def low(value):
    return value.astype(jnp.bfloat16)


def lane_of(shape):
    return lax.broadcasted_iota(jnp.int32, shape, len(shape) - 1)


def mask_to_columns(lo, hi, table):
    out = dot(low(jnp.concatenate([lo + hi, lo - hi], 0)), table[:, :])
    odd = (lane_of((8, 2 * F)) // 16) % 2
    return jnp.where(odd == 0, out[:8], out[8:])


def columns_transposed(got):
    lo, hi = got[:8].reshape(64, 128), got[8:].reshape(64, 128)
    return jnp.concatenate([lo + hi, lo - hi], 0).T


def spectrum(got, table):
    wide = jnp.concatenate([got[k] for k in range(KERNS)], 1)
    first = (lane_of(wide.shape) % 128) < 64
    zero = jnp.zeros_like(wide)
    left = jnp.concatenate([jnp.where(first, wide, zero), jnp.where(first, zero, wide)], 0)
    out = dot(left, table[:, :])
    real, imag = [], []
    for par in range(2):
        part = out[64 * par : 64 * par + 64]
        real.append(part[:32, :EVEN] + part[32:, EVEN:])
        imag.append(part[32:, :EVEN] - part[:32, EVEN:])
    return jnp.concatenate(real, 1), jnp.concatenate(imag, 1)


def filtered(h_re, h_im, s_re, s_im):
    return low(jnp.concatenate([h_re * s_re - h_im * s_im, h_re * s_im + h_im * s_re], 0))


def rows_of(g, table, chunk):
    halves = []
    for par in range(2):
        left = g[:, par * EVEN : par * EVEN + EVEN]
        with_cos = dot(left, table[par * EVEN : par * EVEN + EVEN, chunk * 256 : chunk * 256 + 256])
        with_sin = dot(left, table[par * EVEN : par * EVEN + EVEN, HALF + chunk * 256 : HALF + chunk * 256 + 256])
        halves.append(jnp.concatenate([with_cos[:32] - with_sin[32:], with_cos[32:] + with_sin[:32]], 0))
    return low(halves[0] + halves[1]), low(halves[0] - halves[1])


def turn(block):
    return low(block.astype(jnp.float32).T)


def field(x, table, chunk):
    fields = []
    for par in range(2):
        left = jnp.concatenate(
            [x[:, par * EVEN : par * EVEN + EVEN], x[:, F + par * EVEN : F + par * EVEN + EVEN]], 0
        )
        with_cos = dot(left, table[par * EVEN : par * EVEN + EVEN, chunk * 256 : chunk * 256 + 256])
        with_sin = dot(left, table[par * EVEN : par * EVEN + EVEN, HALF + chunk * 256 : HALF + chunk * 256 + 256])
        fields.append((with_cos[:128] - with_sin[128:], with_cos[128:] + with_sin[:128]))
    (e_re, e_im), (o_re, o_im) = fields
    return (e_re + o_re, e_im + o_im), (e_re - o_re, e_im - o_im)


def light(e):
    power = e[0] * e[0] + e[1] * e[1]
    return jnp.sum(power.reshape(MATES, 16, 256), axis=0)


def sensitivity(intensity, target, doses):
    total = 0.0
    for dose in doses:
        printed = jax.nn.sigmoid(steepness * (dose * intensity - threshold))
        total = total + (printed - target) * printed * (1.0 - printed) * (steepness * dose)
    return total


def cotangent(e, sens):
    spread = jnp.broadcast_to((2.0 * sens)[None], (MATES, 16, 256)).reshape(128, 256)
    return jnp.concatenate([spread * e[0], spread * e[1]], 0)


def back_columns(lo, hi, table, chunk):
    rows = slice(chunk * 256, chunk * 256 + 256)
    return dot(low(lo + hi), table[rows, : 2 * EVEN]), dot(low(lo - hi), table[rows, 2 * EVEN :])


def back_rows(parts):
    real, imag = [], []
    for part in parts:
        real.append(part[:128, :EVEN] + part[128:, EVEN:])
        imag.append(part[128:, :EVEN] - part[:128, EVEN:])
    return low(jnp.concatenate(real + imag, 1))


def grad_spectrum(got, table, h_re, h_im):
    wide = jnp.concatenate([got[s] for s in range(8)], 1).astype(jnp.float32)
    late = jnp.concatenate([got[s] for s in range(8, 16)], 1).astype(jnp.float32)
    real, imag = [], []
    for par, left in enumerate((wide + late, wide - late)):
        out = dot(low(left), table[:, par * 2 * EVEN : (par + 1) * 2 * EVEN])
        real.append(out[:32, :EVEN] + out[32:, EVEN:])
        imag.append(out[32:, :EVEN] - out[:32, EVEN:])
    g_re, g_im = jnp.concatenate(real, 1), jnp.concatenate(imag, 1)
    return low(jnp.concatenate([h_re * g_re + h_im * g_im, h_re * g_im - h_im * g_re], 0))


def adjoint_rows(d, table, roll):
    halves = []
    for par in range(2):
        left = d[:, par * EVEN : par * EVEN + EVEN]
        out = dot(left, table[par * EVEN : par * EVEN + EVEN, :])
        halves.append(
            jnp.concatenate([out[:32, :HALF] - out[32:, HALF:], out[:32, HALF:] + out[32:, :HALF]], 0)
        )
    up, down = halves[0] + halves[1], halves[0] - halves[1]
    first = lane_of((64, 128)) < 64
    blocks = []
    for m in range(8):
        u, v = up[:, 128 * m : 128 * m + 128], down[:, 128 * m : 128 * m + 128]
        blocks.append(low(jnp.where(first, u, roll(v))))
        blocks.append(low(jnp.where(first, roll(u), v)))
    return blocks


def adjoint_sum(got):
    total = jnp.sum(got.astype(jnp.float32), axis=0)
    return jnp.concatenate([total, total], 0).T


def mask_grad(got, table):
    first = lane_of((8, 128)) < 64
    wide = jnp.concatenate([jnp.where(first, got[2 * p], got[2 * p + 1]) for p in range(8)], 1)
    odd = (lane_of(wide.shape) // 16) % 2
    left = jnp.concatenate([jnp.where(odd == 0, wide, 0.0), jnp.where(odd == 0, 0.0, wide)], 0)
    out = dot(low(left), table[:, :])
    return out[:8] + out[8:], out[:8] - out[8:]


def kernel(
    mask_hbm, target_hbm, h_hbm, dose_ref, *rest
):
    table_hbm = rest[:6]
    params_out, light_out = rest[6:8]
    (
        t_in, t_own, t_to, t_from, t_toown, t_mix, h, target, acc, half,
        r0, s1, r1, s2, r2, s3, r3, s4, r4, s5, r5, s6, r6, s7, r7, s8, r8, s9, r9, s10, r10,
        local_sem, send_sem, recv_sem,
    ) = rest[8:]
    me_k, me_s = lax.axis_index("kern"), lax.axis_index("slab")
    mate, focus = me_k // 2, me_k % 2
    vmem_tables = (t_in, t_own, t_to, t_from, t_toown, t_mix)

    loads = [pltpu.make_async_copy(src, dst, local_sem.at[n]) for n, (src, dst) in enumerate(zip(table_hbm, vmem_tables))]
    own_block = pltpu.make_async_copy(mask_hbm.at[pl.ds(pl.multiple_of(8 * me_k, 8), 8)], r0.at[me_k], local_sem.at[6])
    load_h = pltpu.make_async_copy(h_hbm, h, local_sem.at[7])
    load_target = pltpu.make_async_copy(
        target_hbm.at[pl.ds(pl.multiple_of(16 * mate, 16), 16)], target, local_sem.at[8]
    )
    own_block.start()
    loads[0].start()
    loads[1].start()
    load_h.start()
    for n in range(2, 6):
        loads[n].start()
    load_target.start()

    def to_kern(t):
        return (lax.rem(me_k + t, KERNS), me_s)

    def to_slab(t):
        return (me_k, lax.rem(me_s + t, SLABS))

    barrier = pltpu.get_barrier_semaphore()

    def greet(t, carry):
        pl.semaphore_signal(barrier, inc=1, device_id=to_kern(t), device_id_type=MESH)
        pl.semaphore_signal(barrier, inc=1, device_id=to_slab(t), device_id_type=MESH)
        return carry

    lax.fori_loop(1, 16, greet, 0)
    pl.semaphore_wait(barrier, 30)

    def send(phase, src, dst, device):
        pltpu.make_async_remote_copy(
            src_ref=src, dst_ref=dst, send_sem=send_sem.at[phase], recv_sem=recv_sem.at[phase],
            device_id=device, device_id_type=MESH,
        ).start()

    sent = []

    def over_kern(phase, source, dst, size):
        def one(t, carry):
            device = to_kern(t)
            send(phase, source(device[0]), dst.at[me_k], device)
            return carry

        lax.fori_loop(1, KERNS, one, 0, unroll=True)
        sent.append((phase, size))

    def over_slab(phase, source, dst, size):
        def one(t, carry):
            device = to_slab(t)
            send(phase, source(device[1]), dst.at[me_s], device)
            return carry

        lax.fori_loop(1, SLABS, one, 0, unroll=True)
        sent.append((phase, size))

    def over_mates(phase, source, dst, size):
        def one(t, carry):
            other = lax.rem(mate + t, MATES)
            send(phase, source(other), dst.at[mate], (2 * other + focus, me_s))
            return carry

        lax.fori_loop(1, MATES, one, 0, unroll=True)
        sent.append((phase, size))

    def arrive(phase, dst):
        rest_of = dst.at[pl.ds(0, dst.shape[0] - 1)]
        pltpu.make_async_copy(rest_of, rest_of, recv_sem.at[phase]).wait()

    over_kern(0, lambda k: mask_hbm.at[pl.ds(pl.multiple_of(8 * k, 8), 8)], r0, r0)
    own_block.wait()
    arrive(0, r0)
    lo = jnp.concatenate([r0[b] for b in range(8)], 1)
    hi = jnp.concatenate([r0[b] for b in range(8, 16)], 1)

    for step in range(STEPS):
        base = 1 + 8 * step
        b1, b2, b3, b4, b5, b6, b7, b8 = (
            (s.at[step], r.at[step])
            for s, r in ((s1, r1), (s2, r2), (s3, r3), (s4, r4), (s5, r5), (s6, r6), (s7, r7), (s8, r8))
        )
        mask_lo, mask_hi = jnp.tanh(lo), jnp.tanh(hi)
        if step == 0:
            loads[0].wait()
        columns = mask_to_columns(mask_lo, mask_hi, t_in)
        for p in range(8):
            b1[0][p] = columns[:, 128 * p : 128 * p + 128]
        over_slab(base, lambda s: b1[0].at[s // 2], b1[1], b1[1])
        b1[1][me_s] = b1[0][me_s // 2]
        arrive(base, b1[1])

        half[...] = columns_transposed(b1[1][...])
        b2[0][...] = low(half[pl.ds(pl.multiple_of(64 * (me_s % 2), 64), 64), :])
        over_kern(base + 1, lambda k: b2[0], b2[1], b2[1])
        b2[1][me_k] = b2[0][...]
        if step == 0:
            loads[1].wait()
            load_h.wait()
        arrive(base + 1, b2[1])

        s_re, s_im = spectrum(b2[1], t_own)
        g = filtered(h[0], h[1], s_re, s_im)
        if step == 0:
            loads[2].wait()
        for q in range(4):
            first, second = rows_of(g, t_to, q)
            for n in range(2):
                b3[0][2 * q + n] = first[:, 128 * n : 128 * n + 128]
                b3[0][2 * q + n + 8] = second[:, 128 * n : 128 * n + 128]
        over_slab(base + 2, lambda s: b3[0].at[s], b3[1], b3[1])
        b3[1][me_s] = b3[0][me_s]
        arrive(base + 2, b3[1])

        for h8 in range(2):
            for q in range(4):
                block = b3[1][8 * h8 : 8 * h8 + 8, 16 * q : 16 * q + 16, :].reshape(128, 128)
                b4[0][:, 256 * q + 128 * h8 : 256 * q + 128 * h8 + 128] = turn(block)
        over_mates(base + 3, lambda j: b4[0].at[pl.ds(pl.multiple_of(16 * j, 16), 16)], b4[1], b4[1])
        b4[1][mate] = b4[0][pl.ds(pl.multiple_of(16 * mate, 16), 16), :]
        if step == 0:
            loads[3].wait()
            load_target.wait()
        arrive(base + 3, b4[1])

        x = b4[1][...].reshape(128, 2 * F)
        doses = [dose_ref[d] for d in range(2)]
        for q in range(4):
            cots = []
            for n, e in enumerate(field(x, t_to, q)):
                intensity = light(e)
                start = n * HALF + 256 * q
                if step == STEPS - 1:
                    for m in range(2):
                        s9[start // 128 + m] = low(intensity[:, 128 * m : 128 * m + 128])
                sens = sensitivity(intensity, target[:, start : start + 256].astype(jnp.float32), doses)
                cots.append(cotangent(e, sens))
            for par, term in enumerate(back_columns(cots[0], cots[1], t_from, q)):
                if q == 0:
                    acc[par] = term
                else:
                    acc[par] += term
        b5[0][...] = back_rows((acc[0], acc[1])).reshape(MATES, 16, 2 * F)
        over_mates(base + 4, lambda j: b5[0].at[j], b5[1], b5[1])
        b5[1][mate] = b5[0][mate]
        if step == STEPS - 1:
            over_kern(17, lambda k: s9.at[k], r9, r9)
            r9[me_k] = s9[me_k]
        arrive(base + 4, b5[1])

        for h8 in range(2):
            for q in range(4):
                block = b5[1][:, :, 256 * q + 128 * h8 : 256 * q + 128 * h8 + 128].reshape(128, 128)
                b6[0][8 * h8 : 8 * h8 + 8, 16 * q : 16 * q + 16, :] = turn(block).reshape(8, 16, 128)
        over_slab(base + 5, lambda s: b6[0].at[s], b6[1], b6[1])
        b6[1][me_s] = b6[0][me_s]
        arrive(base + 5, b6[1])

        d = grad_spectrum(b6[1], t_from, h[0], h[1])
        if step == 0:
            loads[4].wait()
        for n, block in enumerate(adjoint_rows(d, t_toown, lambda v: pltpu.roll(v, 64, 1))):
            b7[0][n] = block
        over_kern(base + 6, lambda k: b7[0].at[k], b7[1], b7[1])
        b7[1][me_k] = b7[0][me_k]
        arrive(base + 6, b7[1])

        b8[0][...] = adjoint_sum(b7[1][...]).reshape(SLABS, 8, 128)
        over_slab(base + 7, lambda s: b8[0].at[s], b8[1], b8[1])
        b8[1][me_s] = b8[0][me_s]
        if step == 0:
            loads[5].wait()
        arrive(base + 7, b8[1])

        grad_lo, grad_hi = mask_grad(b8[1], t_mix)
        lo = lo - step_rate * grad_lo * (1.0 - mask_lo * mask_lo)
        hi = hi - step_rate * grad_hi * (1.0 - mask_hi * mask_hi)

    for b in range(8):
        s10[b] = lo[:, 128 * b : 128 * b + 128]
        s10[b + 8] = hi[:, 128 * b : 128 * b + 128]
    over_kern(18, lambda k: s10.at[k], r10, r10)
    r10[me_k] = s10[me_k]
    arrive(17, r9)
    for k in range(KERNS):
        light_out[k % 2, 16 * (k // 2) : 16 * (k // 2) + 16, :] = r9[k].astype(jnp.float32)
    arrive(18, r10)
    params_out[...] = r10[...].reshape(128, 128)
    for phase, buffer in sent:
        rest_of = buffer.at[pl.ds(0, buffer.shape[0] - 1)]
        pltpu.make_async_copy(rest_of, rest_of, send_sem.at[phase]).wait()


def body(mask_params, target_bits, kernels, weights, dose_factors):
    scaled = kernels[0] * jnp.sqrt(weights[0])
    h = scaled.reshape(2, EVEN, 2, 16, 2).transpose(0, 4, 3, 2, 1).reshape(2, 32, F)
    f32, bf16 = jnp.float32, jnp.bfloat16
    consts = [jnp.asarray(t) for t in tables()]
    exchange = []
    for shape, send_shape, kind in (
        ((16, 8, 128), (8, 8, 128), f32),
        ((16, 64, 128), (64, 128), bf16),
        ((16, 64, 128), (16, 64, 128), bf16),
        ((8, 16, 1024), (128, 1024), bf16),
        ((8, 16, 1024), (8, 16, 1024), bf16),
        ((16, 64, 128), (16, 64, 128), bf16),
        ((16, 64, 128), (16, 64, 128), bf16),
        ((16, 8, 128), (16, 8, 128), f32),
    ):
        exchange += [pltpu.VMEM((STEPS,) + send_shape, kind), pltpu.VMEM((STEPS,) + shape, kind)]
    hbm, vmem = pl.BlockSpec(memory_space=pl.ANY), pl.BlockSpec(memory_space=pltpu.VMEM)
    params, intensity = pl.pallas_call(
        kernel,
        out_shape=(jax.ShapeDtypeStruct((128, 128), f32), jax.ShapeDtypeStruct((2, 128, 128), f32)),
        in_specs=[hbm, hbm, hbm, pl.BlockSpec(memory_space=pltpu.SMEM)] + [hbm] * 6,
        out_specs=(vmem, vmem),
        scratch_shapes=[pltpu.VMEM(t.shape, bf16) for t in consts]
        + [
            pltpu.VMEM((2, 32, F), f32),
            pltpu.VMEM((16, N), jnp.int32),
            pltpu.VMEM((2, 256, 2 * EVEN), f32),
            pltpu.VMEM((128, 128), f32),
            pltpu.VMEM((16, 8, 128), f32),
        ]
        + exchange
        + [
            pltpu.VMEM((16, 16, 128), bf16),
            pltpu.VMEM((16, 16, 128), bf16),
            pltpu.VMEM((16, 8, 128), f32),
            pltpu.VMEM((16, 8, 128), f32),
            pltpu.SemaphoreType.DMA((9,)),
            pltpu.SemaphoreType.DMA((19,)),
            pltpu.SemaphoreType.DMA((19,)),
        ],
        compiler_params=pltpu.CompilerParams(
            collective_id=0, has_side_effects=True, vmem_limit_bytes=48 * 1024 * 1024
        ),
    )(mask_params, target_bits, h, dose_factors, *consts)
    printed = jax.nn.sigmoid(
        steepness * (dose_factors[None, :, None, None] * intensity[:, None] - threshold)
    )
    return params, printed


def solution(mesh):
    in_specs = (P("slab", "kern"), P("slab", None), P("kern", None, None, "slab"), P("kern"), P())
    out_specs = (P("slab", "kern"), P(None, None, "slab", "kern"))
    return jax.shard_map(body, mesh=mesh, in_specs=in_specs, out_specs=out_specs, check_vma=False)
```

```python
import math

import jax
import jax.numpy as jnp
import ml_dtypes
import numpy as np
from jax import lax
from jax.experimental import pallas as pl
from jax.experimental.pallas import tpu as pltpu
from jax.sharding import PartitionSpec as P

N = 2048
F = 512
STEPS = 2
HALF = N // 2
EVEN = F // 2
KERNS = 16
SLABS = 16
PEERS = 64

steepness = 3.0
threshold = 1.0
step_rate = 0.4
MESH = pl.DeviceIdType.MESH


def tables():
    index = np.concatenate([np.arange(0, F, 2), np.arange(1, F, 2)])
    phases = ((index[:, None] - F // 2) * np.arange(HALF)[None, :]) % N
    angles = phases * (2.0 * math.pi / N)
    scale = 1.0 / math.sqrt(N)
    cos, sin = np.cos(angles) * scale, np.sin(angles) * scale
    y, p, k, i = np.meshgrid(np.arange(2), np.arange(2), np.arange(8), np.arange(16), indexing="ij")
    rows = [((y * 4 + 2 * h + p) * 128 + k * 16 + i).reshape(-1) for h in range(2)]
    to_freq = np.stack([np.concatenate([cos[:, r], sin[:, r]], 1) for r in rows])
    to_rows = to_freq.reshape(2, 2, EVEN, 2, 512).transpose(0, 4, 1, 3, 2).reshape(2, 512, HALF)
    to_cols = np.concatenate([cos, sin], 1)
    from_cols = np.concatenate([cos[:EVEN].T, sin[:EVEN].T, cos[EVEN:].T, sin[EVEN:].T], 1)
    c, s = cos.reshape(2, 4, 64, HALF), sin.reshape(2, 4, 64, HALF)
    mixed = np.stack([c, -s], 2).reshape(2, F, HALF)
    cast = lambda table: np.ascontiguousarray(table).astype(np.float32).astype(ml_dtypes.bfloat16)
    return [cast(t) for t in (mixed.transpose(0, 2, 1), to_freq, to_rows, to_cols, from_cols, mixed)]


def dot(left, right):
    return jnp.dot(left, right, preferred_element_type=jnp.float32)


def low(value):
    return value.astype(jnp.bfloat16)


def wide(value):
    return value.astype(jnp.float32)


def is_real(shape):
    return lax.broadcasted_iota(jnp.int32, shape, len(shape) - 1) < 64


def to_spectrum(got, table, roll):
    lo, hi = wide(got[:512]), wide(got[512:])
    parts = []
    for par, x in enumerate((lo + hi, lo - hi)):
        turned = jnp.where(is_real(x.shape), roll(x), -roll(x))
        both = low(jnp.concatenate([x, turned], 0))
        parts.append(dot(table[par * EVEN : par * EVEN + EVEN, :], both))
    return jnp.concatenate(parts, 0)


def to_pixel_rows(spec, table, roll):
    turned = jnp.where(is_real(spec.shape), -roll(spec), roll(spec))
    parts = []
    for par in range(2):
        rows = slice(par * EVEN, par * EVEN + EVEN)
        both = low(jnp.concatenate([spec[rows], turned[rows]], 0))
        parts.append(dot(table[:, par * F : par * F + F], both))
    return low(parts[0] + parts[1]), low(parts[0] - parts[1])


def pair_in(first, second, roll):
    first, second = wide(first), wide(second)
    real = is_real(first.shape)
    return low(jnp.where(real, first, roll(second))), low(jnp.where(real, roll(first), second))


def pair_out(re, im, roll):
    real = is_real(re.shape)
    return low(jnp.where(real, re, roll(im))), low(jnp.where(real, roll(re), im))


def field(lefts, table, chunk):
    fields = []
    for par, left in enumerate(lefts):
        rows = slice(par * EVEN, par * EVEN + EVEN)
        with_cos = dot(left, table[rows, chunk * 256 : chunk * 256 + 256])
        with_sin = dot(left, table[rows, HALF + chunk * 256 : HALF + chunk * 256 + 256])
        fields.append((with_cos[:128] - with_sin[128:], with_cos[128:] + with_sin[:128]))
    (e_re, e_im), (o_re, o_im) = fields
    return (e_re + o_re, e_im + o_im), (e_re - o_re, e_im - o_im)


def light(e):
    power = e[0] * e[0] + e[1] * e[1]
    return jnp.sum(power.reshape(8, 16, 256), axis=0)


def sensitivity(intensity, target, doses):
    total = 0.0
    for dose in doses:
        printed = jax.nn.sigmoid(steepness * (dose * intensity - threshold))
        total = total + (printed - target) * printed * (1.0 - printed) * (steepness * dose)
    return total


def cotangent(e, sens):
    spread = jnp.broadcast_to((2.0 * sens)[None], (8, 16, 256)).reshape(128, 256)
    return jnp.concatenate([spread * e[0], spread * e[1]], 0)


def back_columns(lo, hi, table, chunk):
    rows = slice(chunk * 256, chunk * 256 + 256)
    return dot(low(lo + hi), table[rows, :F]), dot(low(lo - hi), table[rows, F:])


def back_tiles(part, roll):
    re = part[:128, :EVEN] + part[128:, EVEN:]
    im = part[128:, :EVEN] - part[:128, EVEN:]
    tiles = []
    for m in range(2):
        lanes = slice(128 * m, 128 * m + 128)
        tiles.extend(pair_out(re[:, lanes], im[:, lanes], roll))
    return tiles


def grad_part(got, table):
    blocks = jnp.sum(wide(got).reshape(2, 4, 8, 16, 128), axis=(0, 2))
    return dot(low(jnp.concatenate([blocks[y] for y in range(4)], 1)), table[:, :])


def kernel(mask_hbm, target_hbm, h_hbm, weight_ref, dose_ref, *rest):
    table_hbm = rest[:6]
    params_out, light_out = rest[6:8]
    (
        t_mask, t_freq, t_rows, t_cols, t_back, t_mix,
        h_raw, h_re, h_im, h_turn, target_raw, target, acc,
        r0, hs, hr, ts, tr, s9, r9, s10, r10,
        s_a, r_a, s_sp, r_sp, s_b, r_b, s_db, r_db, s_d, r_d, s_da, r_da, s_g, r_g,
        local_sem, send_sem, recv_sem,
    ) = rest[8:]
    me_k, me_s = lax.axis_index("kern"), lax.axis_index("slab")
    kappa, core = me_k // 2, me_k % 2
    z_lo, x_at = kappa // 4, kappa % 4
    y_at, focus, par = me_s // 4, (me_s % 4) // 2, me_s % 2
    place = y_at * 16 + par * 8 + kappa
    sign = (1 - 2 * core).astype(jnp.float32)
    roll = lambda v: pltpu.roll(v, 64, 1)

    def device(kappa, core, y, focus, par):
        return (2 * kappa + core, 4 * y + 2 * focus + par)

    sibling = (me_k + 1 - 2 * core, me_s)

    own_block = pltpu.make_async_copy(
        mask_hbm.at[pl.ds(pl.multiple_of(16 * kappa, 16), 16)], r0.at[me_k], local_sem.at[6]
    )
    load_target = pltpu.make_async_copy(
        target_hbm.at[pl.ds(pl.multiple_of(16 * kappa, 16), 16)], target_raw, local_sem.at[8]
    )
    loads = [
        pltpu.make_async_copy(table_hbm[0].at[core], t_mask, local_sem.at[0]),
        pltpu.make_async_copy(table_hbm[1].at[core], t_freq, local_sem.at[1]),
        pltpu.make_async_copy(table_hbm[2].at[core], t_rows, local_sem.at[2]),
        pltpu.make_async_copy(table_hbm[3], t_cols, local_sem.at[3]),
        pltpu.make_async_copy(table_hbm[4], t_back, local_sem.at[4]),
        pltpu.make_async_copy(table_hbm[5].at[core], t_mix, local_sem.at[5]),
    ]
    own_block.start()
    for b in range(4):
        pltpu.make_async_copy(h_hbm.at[:, :, pl.ds(128 * b, 128)], h_raw.at[b], local_sem.at[7]).start()
    load_target.start()
    for load in loads:
        load.start()

    barrier = pltpu.get_barrier_semaphore()

    def greet(t, carry):
        slab = lax.rem(me_s + t, SLABS)
        kern = lax.rem(me_k + t, KERNS)
        pl.semaphore_signal(barrier, inc=1, device_id=(me_k, slab), device_id_type=MESH)
        pl.semaphore_signal(barrier, inc=1, device_id=(kern, me_s), device_id_type=MESH)
        return carry

    lax.fori_loop(1, 16, greet, 0)

    pltpu.make_async_copy(h_raw, h_raw, local_sem.at[7]).wait()
    root = jnp.sqrt(jnp.full((16, 128), weight_ref[0], jnp.float32))
    for q in range(2):
        for part in range(2):
            for b in range(4):
                own_rows = h_raw[b, part, pl.ds(q, 16, stride=2), :]
                hs[q, 16 * part : 16 * part + 16, 128 * b : 128 * b + 128] = low(own_rows * root)
    load_target.wait()
    ts[...] = low(wide(target_raw[...]))

    pl.semaphore_wait(barrier, 30)

    sent = []

    def send(phase, src, dst, where):
        pltpu.make_async_remote_copy(
            src_ref=src, dst_ref=dst, send_sem=send_sem.at[phase], recv_sem=recv_sem.at[phase],
            device_id=where, device_id_type=MESH,
        ).start()

    def maybe_own(phase, src, dst, where, is_own):
        if is_own is True:
            pltpu.make_async_copy(src, dst, recv_sem.at[phase]).start()
            return

        @pl.when(is_own)
        def _():
            pltpu.make_async_copy(src, dst, recv_sem.at[phase]).start()

        @pl.when(jnp.logical_not(is_own))
        def _():
            send(phase, src, dst, where)

    def sent_maybe(phase, buffer, is_own):
        @pl.when(jnp.logical_not(is_own))
        def _():
            pltpu.make_async_copy(buffer, buffer, send_sem.at[phase]).wait()

    def take(phase, buffer):
        pltpu.make_async_copy(buffer, buffer, recv_sem.at[phase]).wait()

    def given(phase, buffer):
        pltpu.make_async_copy(buffer, buffer, send_sem.at[phase]).wait()

    def direct(phase, copy, dst, is_own):
        for dx in (2, 1, 3, 0):
            for dy in (2, 1, 3, 0):
                for db, dz in ((1, 1), (1, 0), (0, 1), (0, 0)):
                    to_kappa = lax.rem(z_lo + dz, 2) * 4 + lax.rem(x_at + dx, 4)
                    src, where = copy(to_kappa, lax.rem(y_at + dy, 4), db)
                    if (dx, dy, db, dz) == (0, 0, 0, 0):
                        maybe_own(phase, src, dst, where, is_own)
                    else:
                        send(phase, src, dst, where)
        sent.append((phase, is_own))

    def out_rows(t, carry):
        kern = lax.rem(me_k + t, KERNS)
        send(0, mask_hbm.at[pl.ds(pl.multiple_of(16 * (kern // 2), 16), 16)], r0.at[me_k], (kern, me_s))
        return carry

    lax.fori_loop(1, KERNS, out_rows, 0, unroll=True)
    own_block.wait()
    take(0, r0.at[pl.ds(0, KERNS - 1)])
    lo = jnp.concatenate([r0[b] for b in range(8)], 1)
    hi = jnp.concatenate([r0[b] for b in range(8, 16)], 1)

    own_target = focus == core
    for step in range(STEPS):
        base = 5 + 7 * step
        first, last = step == 0, step == STEPS - 1

        mask_lo, mask_hi = jnp.tanh(lo), jnp.tanh(hi)
        if first:
            loads[0].wait()
        columns = dot(low(mask_lo + sign * mask_hi), t_mask[...])
        for b in range(4):
            s_a[step, b] = low(columns[:, 128 * b : 128 * b + 128])
        direct(
            base,
            lambda k, y, b: (s_a.at[step, y], device(k, focus, y, lax.rem(focus + b, 2), core)),
            r_a.at[step, place],
            (par == core) & (focus == core),
        )
        if first:
            for q in range(2):
                for to_core in range(2):
                    maybe_own(
                        1, hs.at[q], hr.at[me_s % 4], device(kappa, to_core, y_at, core, q),
                        (me_s % 4 == 2 * core + q) & (core == to_core),
                    )

            @pl.when(own_target)
            def _():
                send(2, ts, tr, device(kappa, core, y_at, 1 - focus, par))

            loads[1].wait()
        take(base, r_a.at[step])
        part = to_spectrum(r_a[step].reshape(HALF, 128), t_freq, roll)
        s_sp[step] = low(part)
        send(base + 1, s_sp.at[step], r_sp.at[step], sibling)
        if first:
            take(1, hr)
            flat = jnp.concatenate(
                [hr[z, 16 * c : 16 * c + 16, :] for c in range(2) for z in range(4)], 0
            )
            h_turn[...] = wide(flat).T
            for q in range(2):
                rows = slice(q * EVEN, q * EVEN + EVEN)
                h = h_turn[pl.ds(q, EVEN, stride=2), :]
                turned = roll(h)
                h_re[rows, :] = jnp.where(is_real(h.shape), h, turned)
                h_im[rows, :] = jnp.where(is_real(h.shape), -turned, h)
            loads[2].wait()
        take(base + 1, r_sp.at[step])
        spec = part + wide(r_sp[step])

        filtered = h_re[...] * spec + h_im[...] * roll(spec)
        low_rows, high_rows = to_pixel_rows(filtered, t_rows, roll)
        s_b[step, :32] = low_rows.reshape(32, 16, 128)
        s_b[step, 32:] = high_rows.reshape(32, 16, 128)

        def to_place(k, y, b):
            to_par = lax.rem(par + b, 2)
            return y * 16 + to_par * 8 + k, to_par

        def rows_out(k, y, b):
            at, to_par = to_place(k, y, b)
            return s_b.at[step, at], device(k, core, y, focus, to_par)

        direct(base + 2, rows_out, r_b.at[step, par * 32 + y_at * 8 + kappa], True)
        if first:
            loads[3].wait()
            loads[4].wait()

            @pl.when(own_target)
            def _():
                target[...] = ts[...]

            @pl.when(jnp.logical_not(own_target))
            def _():
                take(2, tr)
                target[...] = tr[...]
        take(base + 2, r_b.at[step])

        lefts = []
        for q in range(2):
            re, im = [], []
            for m in range(2):
                at = 32 * q + 16 * m
                a, b = pair_in(r_b[step, at : at + 8].reshape(128, 128), r_b[step, at + 8 : at + 16].reshape(128, 128), roll)
                re.append(a)
                im.append(b)
            lefts.append(jnp.concatenate([jnp.concatenate(re, 1), jnp.concatenate(im, 1)], 0))
        doses = [dose_ref[d] for d in range(2)]
        for chunk in range(4):
            cots = []
            for n, e in enumerate(field(lefts, t_cols, chunk)):
                intensity = light(e)
                start = n * HALF + 256 * chunk
                if last:
                    for m in range(2):
                        s9[start // 128 + m] = low(intensity[:, 128 * m : 128 * m + 128])
                sens = sensitivity(intensity, wide(target[:, start : start + 256]), doses)
                cots.append(cotangent(e, sens))
            for q, term in enumerate(back_columns(cots[0], cots[1], t_back, chunk)):
                if chunk == 0:
                    acc[q] = term
                else:
                    acc[q] += term
        for q in range(2):
            for y, tile in enumerate(back_tiles(acc[q], roll)):
                at = 32 * q + 8 * y
                s_db[step, at : at + 8] = tile.reshape(8, 16, 128)

        def back_out(k, y, b):
            to_par = lax.rem(par + b, 2)
            return s_db.at[step, to_par * 32 + y * 8 + k], device(k, core, y, focus, to_par)

        direct(base + 3, back_out, r_db.at[step, place], True)
        if last:
            home = 4 * y_at + 2 * core + par
            maybe_own(3, s9.at[me_k], r9.at[focus * 8 + kappa], (me_k, home), own_target)

            def light_home(t, carry):
                kern = lax.rem(me_k + t, KERNS)
                send(3, s9.at[kern], r9.at[focus * 8 + kappa], (kern, home))
                return carry

            lax.fori_loop(1, KERNS, light_home, 0, unroll=True)
        take(base + 3, r_db.at[step])

        g = to_spectrum(r_db[step].reshape(HALF, 128), t_freq, roll)
        part = h_re[...] * g - h_im[...] * roll(g)
        s_d[step] = low(part)
        send(base + 4, s_d.at[step], r_d.at[step], sibling)
        take(base + 4, r_d.at[step])
        low_rows, high_rows = to_pixel_rows(part + wide(r_d[step]), t_rows, roll)
        s_da[step, :32] = low_rows.reshape(32, 16, 128)
        s_da[step, 32:] = high_rows.reshape(32, 16, 128)

        def adjoint_out(k, y, b):
            at, to_par = to_place(k, y, b)
            return s_da.at[step, at], device(k, par, y, core, to_par)

        direct(
            base + 5, adjoint_out, r_da.at[step, focus * 32 + y_at * 8 + kappa], (par == core) & (focus == core)
        )
        if first:
            loads[5].wait()
        take(base + 5, r_da.at[step])

        own = grad_part(r_da[step], t_mix)
        s_g[step] = own
        send(base + 6, s_g.at[step], r_g.at[step], sibling)
        take(base + 6, r_g.at[step])
        other = r_g[step]
        lo = lo - step_rate * (own + other) * (1.0 - mask_lo * mask_lo)
        hi = hi - step_rate * (sign * (own - other)) * (1.0 - mask_hi * mask_hi)

    for b in range(8):
        s10[b] = lo[:, 128 * b : 128 * b + 128]
        s10[b + 8] = hi[:, 128 * b : 128 * b + 128]
    at_home = me_k // 8 == core
    kern = 8 * core + me_k % 8
    maybe_own(4, s10.at[kern], r10.at[kappa], (kern, me_s), at_home)

    def params_home(t, carry):
        kern = 8 * core + lax.rem(me_k + t, 8)
        send(4, s10.at[kern], r10.at[kappa], (kern, me_s))
        return carry

    lax.fori_loop(1, 8, params_home, 0, unroll=True)
    take(3, r9)
    for k in range(KERNS):
        light_out[k // 8, 16 * (k % 8) : 16 * (k % 8) + 16, :] = wide(r9[k])
    take(4, r10)
    params_out[...] = r10[...].reshape(128, 128)

    given(0, r0.at[pl.ds(0, KERNS - 1)])
    for q in range(2):
        for to_core in range(2):
            sent_maybe(1, hs.at[q], (me_s % 4 == 2 * core + q) & (core == to_core))
    sent_maybe(2, ts, jnp.logical_not(own_target))
    given(3, s9.at[pl.ds(0, KERNS - 1)])
    sent_maybe(3, s9.at[0], own_target)
    given(4, s10.at[pl.ds(0, 7)])
    sent_maybe(4, s10.at[0], at_home)
    for phase, is_own in sent:
        given(phase, r_b.at[0, pl.ds(0, PEERS - 1)])
        if is_own is not True:
            sent_maybe(phase, r_b.at[0, 0], is_own)
    for step in range(STEPS):
        given(5 + 7 * step + 1, s_sp.at[step])
        given(5 + 7 * step + 4, s_d.at[step])
        given(5 + 7 * step + 6, s_g.at[step])


def body(mask_params, target_bits, kernels, weights, dose_factors):
    f32, bf16 = jnp.float32, jnp.bfloat16
    consts = [jnp.asarray(t) for t in tables()]
    hbm, vmem = pl.BlockSpec(memory_space=pl.ANY), pl.BlockSpec(memory_space=pltpu.VMEM)
    smem = pl.BlockSpec(memory_space=pltpu.SMEM)
    exchange = []
    for shape, send_shape, kind in (
        ((PEERS, 16, 128), (4, 16, 128), bf16),
        ((F, 128), (F, 128), bf16),
        ((PEERS, 16, 128), (PEERS, 16, 128), bf16),
        ((PEERS, 16, 128), (PEERS, 16, 128), bf16),
        ((F, 128), (F, 128), bf16),
        ((PEERS, 16, 128), (PEERS, 16, 128), bf16),
        ((16, HALF), (16, HALF), f32),
    ):
        exchange += [pltpu.VMEM((STEPS,) + send_shape, kind), pltpu.VMEM((STEPS,) + shape, kind)]
    params, intensity = pl.pallas_call(
        kernel,
        out_shape=(jax.ShapeDtypeStruct((128, 128), f32), jax.ShapeDtypeStruct((2, 128, 128), f32)),
        in_specs=[hbm, hbm, hbm, smem, smem] + [hbm] * 6,
        out_specs=(vmem, vmem),
        scratch_shapes=[
            pltpu.VMEM((HALF, F), bf16),
            pltpu.VMEM((F, HALF), bf16),
            pltpu.VMEM((F, HALF), bf16),
            pltpu.VMEM((F, N), bf16),
            pltpu.VMEM((HALF, HALF), bf16),
            pltpu.VMEM((F, HALF), bf16),
            pltpu.VMEM((4, 2, 32, 128), f32),
            pltpu.VMEM((F, 128), f32),
            pltpu.VMEM((F, 128), f32),
            pltpu.VMEM((F, 128), f32),
            pltpu.VMEM((16, N), jnp.int32),
            pltpu.VMEM((16, N), bf16),
            pltpu.VMEM((2, 256, F), f32),
            pltpu.VMEM((16, 16, 128), f32),
            pltpu.VMEM((2, 32, F), bf16),
            pltpu.VMEM((4, 32, F), bf16),
            pltpu.VMEM((16, N), bf16),
            pltpu.VMEM((16, N), bf16),
            pltpu.VMEM((16, 16, 128), bf16),
            pltpu.VMEM((16, 16, 128), bf16),
            pltpu.VMEM((16, 16, 128), f32),
            pltpu.VMEM((8, 16, 128), f32),
        ]
        + exchange
        + [
            pltpu.SemaphoreType.DMA((9,)),
            pltpu.SemaphoreType.DMA((19,)),
            pltpu.SemaphoreType.DMA((19,)),
        ],
        compiler_params=pltpu.CompilerParams(
            collective_id=0, has_side_effects=True, vmem_limit_bytes=48 * 1024 * 1024
        ),
    )(mask_params, target_bits, kernels[0].transpose(0, 2, 1), weights, dose_factors, *consts)
    printed = jax.nn.sigmoid(
        steepness * (dose_factors[None, :, None, None] * intensity[:, None] - threshold)
    )
    return params, printed


def solution(mesh):
    in_specs = (P("slab", "kern"), P("slab", None), P("kern", None, None, "slab"), P("kern"), P())
    out_specs = (P("slab", "kern"), P(None, None, "slab", "kern"))
    return jax.shard_map(body, mesh=mesh, in_specs=in_specs, out_specs=out_specs, check_vma=False)
```

```python
import math

import jax
import jax.numpy as jnp
import ml_dtypes
import numpy as np
from jax import lax
from jax.experimental import pallas as pl
from jax.experimental.pallas import tpu as pltpu
from jax.sharding import PartitionSpec as P

N = 2048
F = 512
STEPS = 2
HALF = N // 2
EVEN = F // 2
KERNS = 16
SLABS = 16
PEERS = 64

steepness = 3.0
threshold = 1.0
step_rate = 0.4
MESH = pl.DeviceIdType.MESH


def tables():
    index = np.concatenate([np.arange(0, F, 2), np.arange(1, F, 2)])
    phases = ((index[:, None] - F // 2) * np.arange(HALF)[None, :]) % N
    angles = phases * (2.0 * math.pi / N)
    scale = 1.0 / math.sqrt(N)
    cos, sin = np.cos(angles) * scale, np.sin(angles) * scale
    y, p, k, i = np.meshgrid(np.arange(2), np.arange(2), np.arange(8), np.arange(16), indexing="ij")
    rows = [((y * 4 + 2 * h + p) * 128 + k * 16 + i).reshape(-1) for h in range(2)]
    to_freq = np.stack([np.concatenate([cos[:, r], sin[:, r]], 1) for r in rows])
    to_rows = to_freq.reshape(2, 2, EVEN, 2, 512).transpose(0, 4, 1, 3, 2).reshape(2, 512, HALF)
    to_cols = np.concatenate([cos, sin], 1)
    from_cols = np.concatenate([cos[:EVEN].T, sin[:EVEN].T, cos[EVEN:].T, sin[EVEN:].T], 1)
    c, s = cos.reshape(2, 4, 64, HALF), sin.reshape(2, 4, 64, HALF)
    mixed = np.stack([c, -s], 2).reshape(2, F, HALF)
    cast = lambda table: np.ascontiguousarray(table).astype(np.float32).astype(ml_dtypes.bfloat16)
    return [cast(t) for t in (mixed.transpose(0, 2, 1), to_freq, to_rows, to_cols, from_cols, mixed)]


def dot(left, right):
    return jnp.dot(left, right, preferred_element_type=jnp.float32)


def low(value):
    return value.astype(jnp.bfloat16)


def wide(value):
    return value.astype(jnp.float32)


def is_real(shape):
    return lax.broadcasted_iota(jnp.int32, shape, len(shape) - 1) < 64


def to_spectrum(got, table, roll):
    lo, hi = wide(got[:512]), wide(got[512:])
    parts = []
    for par, x in enumerate((lo + hi, lo - hi)):
        turned = jnp.where(is_real(x.shape), roll(x), -roll(x))
        both = low(jnp.concatenate([x, turned], 0))
        parts.append(dot(table[par * EVEN : par * EVEN + EVEN, :], both))
    return jnp.concatenate(parts, 0)


def to_pixel_rows(spec, table, roll):
    turned = jnp.where(is_real(spec.shape), -roll(spec), roll(spec))
    parts = []
    for par in range(2):
        rows = slice(par * EVEN, par * EVEN + EVEN)
        both = low(jnp.concatenate([spec[rows], turned[rows]], 0))
        parts.append(dot(table[:, par * F : par * F + F], both))
    return low(parts[0] + parts[1]), low(parts[0] - parts[1])


def pair_in(first, second, roll):
    first, second = wide(first), wide(second)
    real = is_real(first.shape)
    return low(jnp.where(real, first, roll(second))), low(jnp.where(real, roll(first), second))


def pair_out(re, im, roll):
    real = is_real(re.shape)
    return low(jnp.where(real, re, roll(im))), low(jnp.where(real, roll(re), im))


def field(lefts, table, chunk):
    fields = []
    for par, left in enumerate(lefts):
        rows = slice(par * EVEN, par * EVEN + EVEN)
        with_cos = dot(left, table[rows, chunk * 256 : chunk * 256 + 256])
        with_sin = dot(left, table[rows, HALF + chunk * 256 : HALF + chunk * 256 + 256])
        fields.append((with_cos[:128] - with_sin[128:], with_cos[128:] + with_sin[:128]))
    (e_re, e_im), (o_re, o_im) = fields
    return (e_re + o_re, e_im + o_im), (e_re - o_re, e_im - o_im)


def light(e):
    power = e[0] * e[0] + e[1] * e[1]
    return jnp.sum(power.reshape(8, 16, 256), axis=0)


def sensitivity(intensity, target, doses):
    total = 0.0
    for dose in doses:
        printed = jax.nn.sigmoid(steepness * (dose * intensity - threshold))
        total = total + (printed - target) * printed * (1.0 - printed) * (steepness * dose)
    return total


def cotangent(e, sens):
    spread = jnp.broadcast_to((2.0 * sens)[None], (8, 16, 256)).reshape(128, 256)
    return jnp.concatenate([spread * e[0], spread * e[1]], 0)


def back_columns(lo, hi, table, chunk):
    rows = slice(chunk * 256, chunk * 256 + 256)
    return dot(low(lo + hi), table[rows, :F]), dot(low(lo - hi), table[rows, F:])


def back_tiles(part, roll):
    re = part[:128, :EVEN] + part[128:, EVEN:]
    im = part[128:, :EVEN] - part[:128, EVEN:]
    tiles = []
    for m in range(2):
        lanes = slice(128 * m, 128 * m + 128)
        tiles.extend(pair_out(re[:, lanes], im[:, lanes], roll))
    return tiles


def grad_part(got, table):
    blocks = jnp.sum(wide(got).reshape(2, 4, 8, 16, 128), axis=(0, 2))
    return dot(low(jnp.concatenate([blocks[y] for y in range(4)], 1)), table[:, :])


def kernel(mask_hbm, target_hbm, h_hbm, weight_ref, dose_ref, *rest):
    table_hbm = rest[:6]
    params_out, light_out = rest[6:8]
    (
        t_mask, t_freq, t_rows, t_cols, t_back, t_mix,
        h_raw, h_re, h_im, h_turn, target_raw, target, acc,
        r0, hs, hr, ts, tr, s9, r9, s10, r10,
        s_a, r_a, s_sp, r_sp, s_b, r_b, s_db, r_db, s_d, r_d, s_da, r_da, s_g, r_g,
        local_sem, send_sem, recv_sem,
    ) = rest[8:]
    me_k, me_s = lax.axis_index("kern"), lax.axis_index("slab")
    kappa, core = me_k // 2, me_k % 2
    z_lo, x_at = kappa // 4, kappa % 4
    y_at, focus, par = me_s // 4, (me_s % 4) // 2, me_s % 2
    place = y_at * 16 + par * 8 + kappa
    sign = (1 - 2 * core).astype(jnp.float32)
    roll = lambda v: pltpu.roll(v, 64, 1)

    def device(kappa, core, y, focus, par):
        return (2 * kappa + core, 4 * y + 2 * focus + par)

    sibling = (me_k + 1 - 2 * core, me_s)

    own_block = pltpu.make_async_copy(
        mask_hbm.at[pl.ds(pl.multiple_of(16 * kappa, 16), 16)], r0.at[me_k], local_sem.at[6]
    )
    load_target = pltpu.make_async_copy(
        target_hbm.at[pl.ds(pl.multiple_of(16 * kappa, 16), 16)], target_raw, local_sem.at[8]
    )
    loads = [
        pltpu.make_async_copy(table_hbm[0].at[core], t_mask, local_sem.at[0]),
        pltpu.make_async_copy(table_hbm[1].at[core], t_freq, local_sem.at[1]),
        pltpu.make_async_copy(table_hbm[2].at[core], t_rows, local_sem.at[2]),
        pltpu.make_async_copy(table_hbm[3], t_cols, local_sem.at[3]),
        pltpu.make_async_copy(table_hbm[4], t_back, local_sem.at[4]),
        pltpu.make_async_copy(table_hbm[5].at[core], t_mix, local_sem.at[5]),
    ]
    own_block.start()
    for b in range(4):
        pltpu.make_async_copy(h_hbm.at[:, :, pl.ds(128 * b, 128)], h_raw.at[b], local_sem.at[7]).start()
    load_target.start()
    for load in loads:
        load.start()

    barrier = pltpu.get_barrier_semaphore()

    def greet(t, carry):
        slab = lax.rem(me_s + t, SLABS)
        kern = lax.rem(me_k + t, KERNS)
        pl.semaphore_signal(barrier, inc=1, device_id=(me_k, slab), device_id_type=MESH)
        pl.semaphore_signal(barrier, inc=1, device_id=(kern, me_s), device_id_type=MESH)
        return carry

    lax.fori_loop(1, 16, greet, 0)

    pltpu.make_async_copy(h_raw, h_raw, local_sem.at[7]).wait()
    root = jnp.sqrt(jnp.full((16, 128), weight_ref[0], jnp.float32))
    for q in range(2):
        for part in range(2):
            for b in range(4):
                own_rows = h_raw[b, part, pl.ds(q, 16, stride=2), :]
                hs[q, 16 * part : 16 * part + 16, 128 * b : 128 * b + 128] = low(own_rows * root)
    load_target.wait()
    ts[...] = low(wide(target_raw[...]))

    pl.semaphore_wait(barrier, 30)

    sent = []

    def send(phase, src, dst, where):
        pltpu.make_async_remote_copy(
            src_ref=src, dst_ref=dst, send_sem=send_sem.at[phase], recv_sem=recv_sem.at[phase],
            device_id=where, device_id_type=MESH,
        ).start()

    def maybe_own(phase, src, dst, where, is_own):
        if is_own is True:
            pltpu.make_async_copy(src, dst, recv_sem.at[phase]).start()
            return

        @pl.when(is_own)
        def _():
            pltpu.make_async_copy(src, dst, recv_sem.at[phase]).start()

        @pl.when(jnp.logical_not(is_own))
        def _():
            send(phase, src, dst, where)

    def sent_maybe(phase, buffer, is_own):
        @pl.when(jnp.logical_not(is_own))
        def _():
            pltpu.make_async_copy(buffer, buffer, send_sem.at[phase]).wait()

    def take(phase, buffer):
        pltpu.make_async_copy(buffer, buffer, recv_sem.at[phase]).wait()

    def given(phase, buffer):
        pltpu.make_async_copy(buffer, buffer, send_sem.at[phase]).wait()

    steps_apart = (2, 1, 3, 0)
    nested = [
        (dx, dy, db, dz) for dx in steps_apart for dy in steps_apart for db, dz in ((1, 1), (1, 0), (0, 1), (0, 0))
    ]
    by_distance = sorted(nested, key=lambda d: -(min(d[0], 4 - d[0]) + min(d[1], 4 - d[1]) + 2 * d[2] + d[3]))

    def direct(phase, copy, dst, is_own, order=nested):
        for dx, dy, db, dz in order:
            to_kappa = lax.rem(z_lo + dz, 2) * 4 + lax.rem(x_at + dx, 4)
            src, where = copy(to_kappa, lax.rem(y_at + dy, 4), db)
            if (dx, dy, db, dz) == (0, 0, 0, 0):
                maybe_own(phase, src, dst, where, is_own)
            else:
                send(phase, src, dst, where)
        sent.append((phase, is_own))

    def out_rows(t, carry):
        kern = lax.rem(me_k + t, KERNS)
        send(0, mask_hbm.at[pl.ds(pl.multiple_of(16 * (kern // 2), 16), 16)], r0.at[me_k], (kern, me_s))
        return carry

    lax.fori_loop(1, KERNS, out_rows, 0, unroll=True)

    own_target = focus == core
    for q in range(2):
        maybe_own(
            1, hs.at[q], hr.at[me_s % 4], device(kappa, core, y_at, core, q), me_s % 4 == 2 * core + q
        )

    @pl.when(own_target)
    def _():
        send(2, ts, tr, device(kappa, core, y_at, 1 - focus, par))

    own_block.wait()
    take(0, r0.at[pl.ds(0, KERNS - 1)])
    lo = jnp.concatenate([r0[b] for b in range(8)], 1)
    hi = jnp.concatenate([r0[b] for b in range(8, 16)], 1)

    for step in range(STEPS):
        base = 5 + 7 * step
        first, last = step == 0, step == STEPS - 1

        mask_lo, mask_hi = jnp.tanh(lo), jnp.tanh(hi)
        if first:
            loads[0].wait()
        columns = dot(low(mask_lo + sign * mask_hi), t_mask[...])
        for b in range(4):
            s_a[step, b] = low(columns[:, 128 * b : 128 * b + 128])
        direct(
            base,
            lambda k, y, b: (s_a.at[step, y], device(k, focus, y, lax.rem(focus + b, 2), core)),
            r_a.at[step, place],
            (par == core) & (focus == core),
        )
        if first:

            @pl.when(own_target)
            def _():
                take(1, hr)
                send(19, hr, hr, sibling)

            loads[1].wait()
        take(base, r_a.at[step])
        part = to_spectrum(r_a[step].reshape(HALF, 128), t_freq, roll)
        s_sp[step] = low(part)
        send(base + 1, s_sp.at[step], r_sp.at[step], sibling)
        if first:

            @pl.when(jnp.logical_not(own_target))
            def _():
                take(19, hr)

            flat = jnp.concatenate(
                [hr[z, 16 * c : 16 * c + 16, :] for c in range(2) for z in range(4)], 0
            )
            h_turn[...] = wide(flat).T
            for q in range(2):
                rows = slice(q * EVEN, q * EVEN + EVEN)
                h = h_turn[pl.ds(q, EVEN, stride=2), :]
                turned = roll(h)
                h_re[rows, :] = jnp.where(is_real(h.shape), h, turned)
                h_im[rows, :] = jnp.where(is_real(h.shape), -turned, h)
            loads[2].wait()
        take(base + 1, r_sp.at[step])
        spec = part + wide(r_sp[step])

        filtered = h_re[...] * spec + h_im[...] * roll(spec)
        low_rows, high_rows = to_pixel_rows(filtered, t_rows, roll)
        s_b[step, :32] = low_rows.reshape(32, 16, 128)
        s_b[step, 32:] = high_rows.reshape(32, 16, 128)

        def to_place(k, y, b):
            to_par = lax.rem(par + b, 2)
            return y * 16 + to_par * 8 + k, to_par

        def rows_out(k, y, b):
            at, to_par = to_place(k, y, b)
            return s_b.at[step, at], device(k, core, y, focus, to_par)

        direct(base + 2, rows_out, r_b.at[step, par * 32 + y_at * 8 + kappa], True)
        if first:
            loads[3].wait()
            loads[4].wait()

            @pl.when(own_target)
            def _():
                target[...] = ts[...]

            @pl.when(jnp.logical_not(own_target))
            def _():
                take(2, tr)
                target[...] = tr[...]
        take(base + 2, r_b.at[step])

        lefts = []
        for q in range(2):
            re, im = [], []
            for m in range(2):
                at = 32 * q + 16 * m
                a, b = pair_in(r_b[step, at : at + 8].reshape(128, 128), r_b[step, at + 8 : at + 16].reshape(128, 128), roll)
                re.append(a)
                im.append(b)
            lefts.append(jnp.concatenate([jnp.concatenate(re, 1), jnp.concatenate(im, 1)], 0))
        doses = [dose_ref[d] for d in range(2)]
        for chunk in range(4):
            cots = []
            for n, e in enumerate(field(lefts, t_cols, chunk)):
                intensity = light(e)
                start = n * HALF + 256 * chunk
                if last:
                    for m in range(2):
                        s9[start // 128 + m] = low(intensity[:, 128 * m : 128 * m + 128])
                sens = sensitivity(intensity, wide(target[:, start : start + 256]), doses)
                cots.append(cotangent(e, sens))
            for q, term in enumerate(back_columns(cots[0], cots[1], t_back, chunk)):
                if chunk == 0:
                    acc[q] = term
                else:
                    acc[q] += term
        for q in range(2):
            for y, tile in enumerate(back_tiles(acc[q], roll)):
                at = 32 * q + 8 * y
                s_db[step, at : at + 8] = tile.reshape(8, 16, 128)

        def back_out(k, y, b):
            to_par = lax.rem(par + b, 2)
            return s_db.at[step, to_par * 32 + y * 8 + k], device(k, core, y, focus, to_par)

        direct(base + 3, back_out, r_db.at[step, place], True)
        take(base + 3, r_db.at[step])

        g = to_spectrum(r_db[step].reshape(HALF, 128), t_freq, roll)
        part = h_re[...] * g - h_im[...] * roll(g)
        s_d[step] = low(part)
        send(base + 4, s_d.at[step], r_d.at[step], sibling)
        if last:
            home = 4 * y_at + 2 * core + par
            maybe_own(3, s9.at[me_k], r9.at[focus * 8 + kappa], (me_k, home), own_target)

            def light_home(t, carry):
                kern = lax.rem(me_k + t, KERNS)
                send(3, s9.at[kern], r9.at[focus * 8 + kappa], (kern, home))
                return carry

            lax.fori_loop(1, KERNS, light_home, 0, unroll=True)
        take(base + 4, r_d.at[step])
        low_rows, high_rows = to_pixel_rows(part + wide(r_d[step]), t_rows, roll)
        s_da[step, :32] = low_rows.reshape(32, 16, 128)
        s_da[step, 32:] = high_rows.reshape(32, 16, 128)

        def adjoint_out(k, y, b):
            at, to_par = to_place(k, y, b)
            return s_da.at[step, at], device(k, par, y, core, to_par)

        direct(
            base + 5, adjoint_out, r_da.at[step, focus * 32 + y_at * 8 + kappa], (par == core) & (focus == core),
            by_distance,
        )
        if first:
            loads[5].wait()
        take(base + 5, r_da.at[step])

        own = grad_part(r_da[step], t_mix)
        s_g[step] = own
        send(base + 6, s_g.at[step], r_g.at[step], sibling)
        take(base + 6, r_g.at[step])
        other = r_g[step]
        lo = lo - step_rate * (own + other) * (1.0 - mask_lo * mask_lo)
        hi = hi - step_rate * (sign * (own - other)) * (1.0 - mask_hi * mask_hi)

    for b in range(8):
        s10[b] = lo[:, 128 * b : 128 * b + 128]
        s10[b + 8] = hi[:, 128 * b : 128 * b + 128]
    at_home = me_k // 8 == core
    kern = 8 * core + me_k % 8
    maybe_own(4, s10.at[kern], r10.at[kappa], (kern, me_s), at_home)

    def params_home(t, carry):
        kern = 8 * core + lax.rem(me_k + t, 8)
        send(4, s10.at[kern], r10.at[kappa], (kern, me_s))
        return carry

    lax.fori_loop(1, 8, params_home, 0, unroll=True)
    take(3, r9)
    for k in range(KERNS):
        light_out[k // 8, 16 * (k % 8) : 16 * (k % 8) + 16, :] = wide(r9[k])
    take(4, r10)
    params_out[...] = r10[...].reshape(128, 128)

    given(0, r0.at[pl.ds(0, KERNS - 1)])
    for q in range(2):
        sent_maybe(1, hs.at[q], me_s % 4 == 2 * core + q)
    sent_maybe(19, hr, jnp.logical_not(own_target))
    sent_maybe(2, ts, jnp.logical_not(own_target))
    given(3, s9.at[pl.ds(0, KERNS - 1)])
    sent_maybe(3, s9.at[0], own_target)
    given(4, s10.at[pl.ds(0, 7)])
    sent_maybe(4, s10.at[0], at_home)
    for phase, is_own in sent:
        given(phase, r_b.at[0, pl.ds(0, PEERS - 1)])
        if is_own is not True:
            sent_maybe(phase, r_b.at[0, 0], is_own)
    for step in range(STEPS):
        given(5 + 7 * step + 1, s_sp.at[step])
        given(5 + 7 * step + 4, s_d.at[step])
        given(5 + 7 * step + 6, s_g.at[step])


def body(mask_params, target_bits, kernels, weights, dose_factors):
    f32, bf16 = jnp.float32, jnp.bfloat16
    consts = [jnp.asarray(t) for t in tables()]
    hbm, vmem = pl.BlockSpec(memory_space=pl.ANY), pl.BlockSpec(memory_space=pltpu.VMEM)
    smem = pl.BlockSpec(memory_space=pltpu.SMEM)
    exchange = []
    for shape, send_shape, kind in (
        ((PEERS, 16, 128), (4, 16, 128), bf16),
        ((F, 128), (F, 128), bf16),
        ((PEERS, 16, 128), (PEERS, 16, 128), bf16),
        ((PEERS, 16, 128), (PEERS, 16, 128), bf16),
        ((F, 128), (F, 128), bf16),
        ((PEERS, 16, 128), (PEERS, 16, 128), bf16),
        ((16, HALF), (16, HALF), f32),
    ):
        exchange += [pltpu.VMEM((STEPS,) + send_shape, kind), pltpu.VMEM((STEPS,) + shape, kind)]
    params, intensity = pl.pallas_call(
        kernel,
        out_shape=(jax.ShapeDtypeStruct((128, 128), f32), jax.ShapeDtypeStruct((2, 128, 128), f32)),
        in_specs=[hbm, hbm, hbm, smem, smem] + [hbm] * 6,
        out_specs=(vmem, vmem),
        scratch_shapes=[
            pltpu.VMEM((HALF, F), bf16),
            pltpu.VMEM((F, HALF), bf16),
            pltpu.VMEM((F, HALF), bf16),
            pltpu.VMEM((F, N), bf16),
            pltpu.VMEM((HALF, HALF), bf16),
            pltpu.VMEM((F, HALF), bf16),
            pltpu.VMEM((4, 2, 32, 128), f32),
            pltpu.VMEM((F, 128), f32),
            pltpu.VMEM((F, 128), f32),
            pltpu.VMEM((F, 128), f32),
            pltpu.VMEM((16, N), jnp.int32),
            pltpu.VMEM((16, N), bf16),
            pltpu.VMEM((2, 256, F), f32),
            pltpu.VMEM((16, 16, 128), f32),
            pltpu.VMEM((2, 32, F), bf16),
            pltpu.VMEM((4, 32, F), bf16),
            pltpu.VMEM((16, N), bf16),
            pltpu.VMEM((16, N), bf16),
            pltpu.VMEM((16, 16, 128), bf16),
            pltpu.VMEM((16, 16, 128), bf16),
            pltpu.VMEM((16, 16, 128), f32),
            pltpu.VMEM((8, 16, 128), f32),
        ]
        + exchange
        + [
            pltpu.SemaphoreType.DMA((9,)),
            pltpu.SemaphoreType.DMA((20,)),
            pltpu.SemaphoreType.DMA((20,)),
        ],
        compiler_params=pltpu.CompilerParams(
            collective_id=0, has_side_effects=True, vmem_limit_bytes=62 * 1024 * 1024
        ),
    )(mask_params, target_bits, kernels[0].transpose(0, 2, 1), weights, dose_factors, *consts)
    printed = jax.nn.sigmoid(
        steepness * (dose_factors[None, :, None, None] * intensity[:, None] - threshold)
    )
    return params, printed


def solution(mesh):
    in_specs = (P("slab", "kern"), P("slab", None), P("kern", None, None, "slab"), P("kern"), P())
    out_specs = (P("slab", "kern"), P(None, None, "slab", "kern"))
    return jax.shard_map(body, mesh=mesh, in_specs=in_specs, out_specs=out_specs, check_vma=False)
```

```python
import math

import jax
import jax.numpy as jnp
import ml_dtypes
import numpy as np
from jax import lax
from jax.experimental import pallas as pl
from jax.experimental.pallas import tpu as pltpu
from jax.sharding import PartitionSpec as P

N = 2048
F = 512
STEPS = 2
HALF = N // 2
EVEN = F // 2
KERNS = 16
SLABS = 16
PEERS = 64

steepness = 3.0
threshold = 1.0
step_rate = 0.4
MESH = pl.DeviceIdType.MESH


def tables():
    scale = 1.0 / math.sqrt(N)

    def waves(index):
        phases = ((index[:, None] - F // 2) * np.arange(HALF)[None, :]) % N
        angles = phases * (2.0 * math.pi / N)
        return np.cos(angles) * scale, np.sin(angles) * scale

    cos, sin = waves(np.concatenate([np.arange(0, F, 2), np.arange(1, F, 2)]))
    y, z, k, i = np.meshgrid(np.arange(2), np.arange(2), np.arange(8), np.arange(16), indexing="ij")
    rows = [((y * 4 + 2 * h + z) * 128 + k * 16 + i).reshape(-1) for h in range(2)]
    both = np.stack([cos.reshape(2, EVEN, HALF), sin.reshape(2, EVEN, HALF)], 1).reshape(2 * F, HALF)
    to_rows = np.stack([both[:, r].T for r in rows])
    to_freq = to_rows.transpose(0, 2, 1).reshape(2, 2 * F, 32, 2, 8).transpose(0, 1, 3, 2, 4).reshape(2, 2 * F, 512)
    p, y, z, h, t = np.meshgrid(
        np.arange(2), np.arange(4), np.arange(2), np.arange(2), np.arange(16), indexing="ij"
    )
    cos, sin = waves((32 * (4 * y + 2 * h + z) + 2 * t + p).reshape(-1))
    to_cols = np.concatenate([cos, sin], 1)
    from_cols = np.concatenate([cos[:EVEN].T, sin[:EVEN].T, cos[EVEN:].T, sin[EVEN:].T], 1)
    c, s = cos.reshape(2, 8, 32, HALF), sin.reshape(2, 8, 32, HALF)
    mixed = np.stack([c, -s], 2).reshape(2, F, HALF)
    cast = lambda table: np.ascontiguousarray(table).astype(np.float32).astype(ml_dtypes.bfloat16)
    return [cast(t) for t in (mixed.transpose(0, 2, 1), to_freq, to_rows, to_cols, from_cols, mixed)]


def dot(left, right):
    return jnp.dot(left, right, preferred_element_type=jnp.float32)


def low(value):
    return value.astype(jnp.bfloat16)


def wide(value):
    return value.astype(jnp.float32)


def lane(value):
    return lax.broadcasted_iota(jnp.int32, value.shape, len(value.shape) - 1)


def is_front(value):
    return lane(value) < 64


def is_real(value):
    return lane(value) % 64 < 32


def roll(value, by):
    return pltpu.roll(value, by, 1)


def swap(value):
    return jnp.where(is_real(value), roll(value, 96), roll(value, 32))


def fronts(first, second):
    front = is_front(first)
    return jnp.where(front, first, roll(second, 64)), jnp.where(front, roll(first, 64), second)


def columns_spectrum(got, table):
    lo, hi = wide(got[:32].reshape(256, 128)), wide(got[32:].reshape(256, 128))
    parts = []
    for par, x in enumerate((lo + hi, lo - hi)):
        turned = jnp.where(is_real(x), swap(x), -swap(x))
        front = is_front(x)
        both = jnp.concatenate(
            [jnp.where(front, x, roll(turned, 64)), jnp.where(front, roll(x, 64), turned)], 0
        )
        out = dot(table[par * F : par * F + F, :], low(both))
        one = jnp.where(is_front(out[:EVEN]), out[:EVEN], out[EVEN:])
        parts.append(one + roll(one, 64))
    return jnp.concatenate(parts, 0)


def rows_spectrum(got, table):
    lo, hi = wide(got[:32]), wide(got[32:])
    parts = []
    for par, x in enumerate((lo + hi, lo - hi)):
        x = jnp.concatenate([x[:, :8].reshape(256, 128), x[:, 8:].reshape(256, 128)], 0)
        turned = jnp.where(is_real(x), swap(x), -swap(x))
        at = par * F
        parts.append(dot(table[at : at + EVEN, :], low(x)) + dot(table[at + EVEN : at + F, :], low(turned)))
    return jnp.concatenate(parts, 0)


def pixel_rows(spec, table):
    turned = jnp.where(is_real(spec), -swap(spec), swap(spec))
    parts = []
    for par in range(2):
        rows = slice(par * EVEN, par * EVEN + EVEN)
        both = low(jnp.concatenate([spec[rows], turned[rows]], 0))
        parts.append(dot(table[:, par * F : par * F + F], both))
    return parts[0] + parts[1], parts[0] - parts[1]


def side_by_side(rows):
    rows = rows.reshape(32, 2, 8, 128)
    return low(jnp.where(is_front(rows[:, 0]), rows[:, 0], rows[:, 1]))


def regroup(tiles):
    a, c = fronts(tiles[0], tiles[2])
    b, d = fronts(tiles[1], tiles[3])
    out = []
    for p, q in ((a, b), (c, d)):
        real = is_real(p)
        out += [jnp.where(real, p, roll(q, 32)), jnp.where(real, roll(p, 96), q)]
    return out


def field(lefts, table, chunk):
    fields = []
    for par, left in enumerate(lefts):
        rows = slice(par * EVEN, par * EVEN + EVEN)
        with_cos = dot(left, table[rows, chunk * 256 : chunk * 256 + 256])
        with_sin = dot(left, table[rows, HALF + chunk * 256 : HALF + chunk * 256 + 256])
        fields.append((with_cos[:128] - with_sin[128:], with_cos[128:] + with_sin[:128]))
    (e_re, e_im), (o_re, o_im) = fields
    return (e_re + o_re, e_im + o_im), (e_re - o_re, e_im - o_im)


def light(e):
    power = e[0] * e[0] + e[1] * e[1]
    return jnp.sum(power.reshape(8, 16, 256), axis=0)


def sensitivity(intensity, target, doses):
    total = 0.0
    for dose in doses:
        printed = jax.nn.sigmoid(steepness * (dose * intensity - threshold))
        total = total + (printed - target) * printed * (1.0 - printed) * (steepness * dose)
    return total


def cotangent(e, sens):
    spread = jnp.broadcast_to((2.0 * sens)[None], (8, 16, 256)).reshape(128, 256)
    return jnp.concatenate([spread * e[0], spread * e[1]], 0)


def back_columns(lo, hi, table, chunk):
    rows = slice(chunk * 256, chunk * 256 + 256)
    return dot(low(lo + hi), table[rows, :F]), dot(low(lo - hi), table[rows, F:])


def back_parts(part):
    return part[:128, :EVEN] + part[128:, EVEN:], part[128:, :EVEN] - part[:128, EVEN:]


def grad_part(got, table):
    blocks = jnp.sum(wide(got).reshape(8, 8, 8, 128), axis=1)
    tiles = [jnp.concatenate(fronts(blocks[2 * j], blocks[2 * j + 1]), 0) for j in range(4)]
    return dot(low(jnp.concatenate(tiles, 1)), table[:, :])


def kernel(mask_hbm, target_hbm, h_hbm, weight_ref, dose_ref, *rest):
    table_hbm = rest[:6]
    params_out, light_out = rest[6:8]
    (
        t_mask, t_freq_a, t_freq_b, t_rows_a, t_rows_b, t_cols, t_back, t_mix,
        h_raw, h_re, h_im, h_turn, target, acc,
        r0, hs, hr, s9, r9, s10, r10,
        s_a, r_a, s_sp, r_sp, s_b, r_b, s_db, r_db, s_d, r_d, s_da, r_da, s_g, r_g,
        local_sem, send_sem, recv_sem,
    ) = rest[8:]
    me_k, me_s = lax.axis_index("kern"), lax.axis_index("slab")
    kappa, core = me_k // 2, me_k % 2
    z0, x_at = kappa // 4, kappa % 4
    y_at, z2, z1 = me_s // 4, (me_s % 4) // 2, me_s % 2
    place = y_at * 16 + z1 * 8 + kappa
    block = 2 * y_at + z1
    sign = (1 - 2 * core).astype(jnp.float32)

    def device(x, y, z2, z1, z0, core):
        return (2 * (4 * z0 + x) + core, 4 * y + 2 * z2 + z1)

    sibling = (me_k + 1 - 2 * core, me_s)

    barrier = pltpu.get_barrier_semaphore()

    def greet(t, carry):
        slab = lax.rem(me_s + t, SLABS)
        kern = lax.rem(me_k + t, KERNS)
        pl.semaphore_signal(barrier, inc=1, device_id=(me_k, slab), device_id_type=MESH)
        pl.semaphore_signal(barrier, inc=1, device_id=(kern, me_s), device_id_type=MESH)
        return carry

    pl.semaphore_signal(
        barrier, inc=1, device_id=device(x_at, y_at, 1 - z2, z1, 1 - z0, core), device_id_type=MESH
    )
    lax.fori_loop(1, 16, greet, 0)

    own_block = pltpu.make_async_copy(
        mask_hbm.at[pl.ds(pl.multiple_of(16 * kappa, 16), 16)], r0.at[me_k], local_sem.at[8]
    )
    load_target = pltpu.make_async_copy(
        target_hbm.at[pl.ds(pl.multiple_of(16 * kappa, 16), 16)], target, local_sem.at[9]
    )
    loads = [
        pltpu.make_async_copy(src, dst, local_sem.at[n])
        for n, (src, dst) in enumerate(
            (
                (table_hbm[0].at[core], t_mask),
                (table_hbm[1].at[core], t_freq_a),
                (table_hbm[2].at[z2], t_rows_b),
                (table_hbm[3], t_cols),
                (table_hbm[4], t_back),
                (table_hbm[1].at[z2], t_freq_b),
                (table_hbm[2].at[core], t_rows_a),
                (table_hbm[5].at[core], t_mix),
            )
        )
    ]
    own_block.start()
    for b in range(4):
        pltpu.make_async_copy(h_hbm.at[:, :, pl.ds(128 * b, 128)], h_raw.at[b], local_sem.at[10]).start()
    for load in loads:
        load.start()
    load_target.start()

    pltpu.make_async_copy(h_raw, h_raw, local_sem.at[10]).wait()
    root = jnp.sqrt(jnp.full((16, 128), weight_ref[0], jnp.float32))
    for q in range(2):
        for part in range(2):
            for b in range(4):
                own_rows = h_raw[b, part, pl.ds(q, 16, stride=2), :]
                hs[q, 16 * part : 16 * part + 16, 128 * b : 128 * b + 128] = low(own_rows * root)

    pl.semaphore_wait(barrier, 31)

    sent = []

    def send(phase, src, dst, where):
        pltpu.make_async_remote_copy(
            src_ref=src, dst_ref=dst, send_sem=send_sem.at[phase], recv_sem=recv_sem.at[phase],
            device_id=where, device_id_type=MESH,
        ).start()

    def maybe_own(phase, src, dst, where, is_own):
        if is_own is True:
            pltpu.make_async_copy(src, dst, recv_sem.at[phase]).start()
            return

        @pl.when(is_own)
        def _():
            pltpu.make_async_copy(src, dst, recv_sem.at[phase]).start()

        @pl.when(jnp.logical_not(is_own))
        def _():
            send(phase, src, dst, where)

    def sent_maybe(phase, buffer, is_own):
        @pl.when(jnp.logical_not(is_own))
        def _():
            pltpu.make_async_copy(buffer, buffer, send_sem.at[phase]).wait()

    def take(phase, buffer):
        pltpu.make_async_copy(buffer, buffer, recv_sem.at[phase]).wait()

    def given(phase, buffer):
        pltpu.make_async_copy(buffer, buffer, send_sem.at[phase]).wait()

    steps_apart = (2, 1, 3, 0)
    nested = [
        (dx, dy, da, db) for dx in steps_apart for dy in steps_apart for da, db in ((1, 1), (1, 0), (0, 1), (0, 0))
    ]

    def direct(phase, copy, dst, is_own):
        for dx, dy, da, db in nested:
            src, where = copy(lax.rem(x_at + dx, 4), lax.rem(y_at + dy, 4), da, db)
            if (dx, dy, da, db) == (0, 0, 0, 0):
                maybe_own(phase, src, dst, where, is_own)
            else:
                send(phase, src, dst, where)
        sent.append((phase, is_own))

    def flip(bit, by):
        return 1 - bit if by else bit

    def out_rows(t, carry):
        kern = lax.rem(me_k + t, KERNS)
        send(0, mask_hbm.at[pl.ds(pl.multiple_of(16 * (kern // 2), 16), 16)], r0.at[me_k], (kern, me_s))
        return carry

    lax.fori_loop(1, KERNS, out_rows, 0, unroll=True)

    for dq, dz in ((1, 1), (0, 1), (1, 0), (0, 0)):
        to_par = flip(z0, dq)
        where = device(x_at, y_at, flip(z2, dz), z1, to_par, core)
        if dq or dz:
            send(1, hs.at[to_par], hr.at[2 * z0 + z2], where)
        else:
            maybe_own(1, hs.at[to_par], hr.at[2 * z0 + z2], where, True)

    own_block.wait()
    take(0, r0.at[pl.ds(0, KERNS - 1)])
    lo = jnp.concatenate([r0[b] for b in range(8)], 1)
    hi = jnp.concatenate([r0[b] for b in range(8, 16)], 1)

    owner_is_reader = (z0 == core) & (z2 == core)
    for step in range(STEPS):
        base = 5 + 7 * step
        first, last = step == 0, step == STEPS - 1

        mask_lo, mask_hi = jnp.tanh(lo), jnp.tanh(hi)
        if first:
            loads[0].wait()
        columns = dot(low(mask_lo + sign * mask_hi), t_mask[...])
        for j in range(4):
            tile = columns[:, 128 * j : 128 * j + 128]
            front, back = fronts(tile[:8], tile[8:])
            s_a[step, 2 * j] = low(front)
            s_a[step, 2 * j + 1] = low(back)

        def columns_out(x, y, da, db):
            to_z1 = flip(z1, db)
            return s_a.at[step, 2 * y + to_z1], device(x, y, flip(z2, da), to_z1, core, z2)

        direct(base, columns_out, r_a.at[step, place], owner_is_reader)
        if first:
            loads[1].wait()
        take(base, r_a.at[step])
        part = columns_spectrum(r_a[step], t_freq_a)
        s_sp[step] = low(part)
        send(base + 1, s_sp.at[step], r_sp.at[step], sibling)
        if first:
            take(1, hr)
            flat = jnp.concatenate(
                [hr[2 * k + h, 16 * c : 16 * c + 16, :] for k in range(2) for c in range(2) for h in range(2)], 0
            )
            h_turn[...] = wide(flat).T
            for q in range(2):
                rows = slice(q * EVEN, q * EVEN + EVEN)
                h = h_turn[pl.ds(q, EVEN, stride=2), :]
                swapped = swap(h)
                h_re[rows, :] = jnp.where(is_real(h), h, swapped)
                h_im[rows, :] = jnp.where(is_real(h), -swapped, h)
            loads[2].wait()
        take(base + 1, r_sp.at[step])
        spec = part + wide(r_sp[step])

        filtered = h_re[...] * spec + h_im[...] * swap(spec)
        low_rows, high_rows = pixel_rows(filtered, t_rows_b)
        s_b[step, :32] = low(low_rows).reshape(32, 16, 128)
        s_b[step, 32:] = low(high_rows).reshape(32, 16, 128)

        def rows_out(x, y, da, db):
            to_z1, to_z0 = flip(z1, da), flip(z0, db)
            return s_b.at[step, y * 16 + to_z1 * 8 + to_z0 * 4 + x], device(x, y, z2, to_z1, to_z0, core)

        direct(base + 2, rows_out, r_b.at[step, z0 * 32 + block * 4 + x_at], True)
        if first:
            loads[3].wait()
            loads[4].wait()
            load_target.wait()
        take(base + 2, r_b.at[step])

        lefts = []
        for q in range(2):
            groups = []
            for m in range(2):
                tiles = [32 * q + 16 * m + 4 * g for g in range(4)]
                groups.append(regroup([wide(r_b[step, at : at + 4]).reshape(64, 128) for at in tiles]))
            order = [jnp.concatenate([groups[0][n], groups[1][n]], 1) for n in (0, 2, 1, 3)]
            lefts.append(low(jnp.concatenate(order, 0)))
        doses = [dose_ref[d] for d in range(2)]
        for chunk in range(4):
            cots = []
            for n, e in enumerate(field(lefts, t_cols, chunk)):
                intensity = light(e)
                start = n * HALF + 256 * chunk
                if last:
                    for m in range(2):
                        s9[start // 128 + m] = low(intensity[:, 128 * m : 128 * m + 128])
                sens = sensitivity(intensity, wide(target[:, start : start + 256]), doses)
                cots.append(cotangent(e, sens))
            for q, term in enumerate(back_columns(cots[0], cots[1], t_back, chunk)):
                if chunk == 0:
                    acc[q] = term
                else:
                    acc[q] += term
        for q in range(2):
            re, im = back_parts(acc[q])
            for m in range(2):
                lanes = slice(128 * m, 128 * m + 128)
                tiles = regroup([re[:64, lanes], im[:64, lanes], re[64:, lanes], im[64:, lanes]])
                for g, tile in enumerate(tiles):
                    at = 32 * q + 16 * m + 4 * g
                    s_db[step, at : at + 4] = low(tile).reshape(4, 16, 128)

        def back_out(x, y, da, db):
            to_z1, to_z0 = flip(z1, da), flip(z0, db)
            return s_db.at[step, to_z0 * 32 + (2 * y + to_z1) * 4 + x], device(x, y, z2, to_z1, to_z0, core)

        direct(base + 3, back_out, r_db.at[step, place], True)
        if first:
            loads[5].wait()
        take(base + 3, r_db.at[step])

        g = rows_spectrum(r_db[step], t_freq_b)
        part = h_re[...] * g - h_im[...] * swap(g)
        part = part + roll(part, 64)
        s_d[step] = low(part)
        send(base + 4, s_d.at[step], r_d.at[step], sibling)
        if first:
            loads[6].wait()
        if last:
            maybe_own(3, s9.at[me_k], r9.at[core * 8 + kappa], (me_k, me_s), True)

            def light_home(t, carry):
                kern = lax.rem(me_k + t, KERNS)
                send(3, s9.at[kern], r9.at[core * 8 + kappa], (kern, me_s))
                return carry

            lax.fori_loop(1, KERNS, light_home, 0, unroll=True)
        take(base + 4, r_d.at[step])
        low_rows, high_rows = pixel_rows(part + wide(r_d[step]), t_rows_a)
        s_da[step, :32] = side_by_side(low_rows)
        s_da[step, 32:] = side_by_side(high_rows)

        def adjoint_out(x, y, da, db):
            to_z1, to_z0 = flip(z1, da), flip(z0, db)
            return s_da.at[step, y * 16 + to_z1 * 8 + to_z0 * 4 + x], device(x, y, core, to_z1, to_z0, z0)

        direct(base + 5, adjoint_out, r_da.at[step, block * 8 + z2 * 4 + x_at], owner_is_reader)
        if first:
            loads[7].wait()
        take(base + 5, r_da.at[step])

        own = grad_part(r_da[step], t_mix)
        s_g[step] = own
        send(base + 6, s_g.at[step], r_g.at[step], sibling)
        take(base + 6, r_g.at[step])
        other = r_g[step]
        lo = lo - step_rate * (own + other) * (1.0 - mask_lo * mask_lo)
        hi = hi - step_rate * (sign * (own - other)) * (1.0 - mask_hi * mask_hi)

    for b in range(8):
        s10[b] = lo[:, 128 * b : 128 * b + 128]
        s10[b + 8] = hi[:, 128 * b : 128 * b + 128]
    at_home = me_k // 8 == core
    kern = 8 * core + me_k % 8
    maybe_own(4, s10.at[kern], r10.at[kappa], (kern, me_s), at_home)

    def params_home(t, carry):
        kern = 8 * core + lax.rem(me_k + t, 8)
        send(4, s10.at[kern], r10.at[kappa], (kern, me_s))
        return carry

    lax.fori_loop(1, 8, params_home, 0, unroll=True)
    take(3, r9)
    for k in range(KERNS):
        light_out[k // 8, 16 * (k % 8) : 16 * (k % 8) + 16, :] = wide(r9[k])
    take(4, r10)
    params_out[...] = r10[...].reshape(128, 128)

    given(0, r0.at[pl.ds(0, KERNS - 1)])
    given(1, hr.at[pl.ds(0, 3)])
    given(3, s9.at[pl.ds(0, KERNS - 1)])
    given(4, s10.at[pl.ds(0, 7)])
    sent_maybe(4, s10.at[0], at_home)
    for phase, is_own in sent:
        if is_own is True:
            given(phase, r_b.at[0, pl.ds(0, PEERS - 1)])
        else:
            given(phase, r_a.at[0, pl.ds(0, PEERS - 1)])
            sent_maybe(phase, r_a.at[0, 0], is_own)
    for step in range(STEPS):
        given(5 + 7 * step + 1, s_sp.at[step])
        given(5 + 7 * step + 4, s_d.at[step])
        given(5 + 7 * step + 6, s_g.at[step])


def body(mask_params, target_bits, kernels, weights, dose_factors):
    f32, bf16 = jnp.float32, jnp.bfloat16
    consts = [jnp.asarray(t) for t in tables()]
    hbm, vmem = pl.BlockSpec(memory_space=pl.ANY), pl.BlockSpec(memory_space=pltpu.VMEM)
    smem = pl.BlockSpec(memory_space=pltpu.SMEM)
    exchange = []
    for shape, send_shape, kind in (
        ((PEERS, 8, 128), (8, 8, 128), bf16),
        ((F, 128), (F, 128), bf16),
        ((PEERS, 16, 128), (PEERS, 16, 128), bf16),
        ((PEERS, 16, 128), (PEERS, 16, 128), bf16),
        ((F, 128), (F, 128), bf16),
        ((PEERS, 8, 128), (PEERS, 8, 128), bf16),
        ((16, HALF), (16, HALF), f32),
    ):
        exchange += [pltpu.VMEM((STEPS,) + send_shape, kind), pltpu.VMEM((STEPS,) + shape, kind)]
    params, intensity = pl.pallas_call(
        kernel,
        out_shape=(jax.ShapeDtypeStruct((128, 128), f32), jax.ShapeDtypeStruct((2, 128, 128), f32)),
        in_specs=[hbm, hbm, hbm, smem, smem] + [hbm] * 6,
        out_specs=(vmem, vmem),
        scratch_shapes=[
            pltpu.VMEM((HALF, F), bf16),
            pltpu.VMEM((HALF, F), bf16),
            pltpu.VMEM((HALF, F), bf16),
            pltpu.VMEM((F, HALF), bf16),
            pltpu.VMEM((F, HALF), bf16),
            pltpu.VMEM((F, N), bf16),
            pltpu.VMEM((HALF, HALF), bf16),
            pltpu.VMEM((F, HALF), bf16),
            pltpu.VMEM((4, 2, 32, 128), f32),
            pltpu.VMEM((F, 128), f32),
            pltpu.VMEM((F, 128), f32),
            pltpu.VMEM((F, 128), f32),
            pltpu.VMEM((16, N), jnp.int32),
            pltpu.VMEM((2, 256, F), f32),
            pltpu.VMEM((16, 16, 128), f32),
            pltpu.VMEM((2, 32, F), bf16),
            pltpu.VMEM((4, 32, F), bf16),
            pltpu.VMEM((16, 16, 128), bf16),
            pltpu.VMEM((16, 16, 128), bf16),
            pltpu.VMEM((16, 16, 128), f32),
            pltpu.VMEM((8, 16, 128), f32),
        ]
        + exchange
        + [
            pltpu.SemaphoreType.DMA((11,)),
            pltpu.SemaphoreType.DMA((19,)),
            pltpu.SemaphoreType.DMA((19,)),
        ],
        compiler_params=pltpu.CompilerParams(
            collective_id=0, has_side_effects=True, vmem_limit_bytes=62 * 1024 * 1024
        ),
    )(mask_params, target_bits, kernels[0].transpose(0, 2, 1), weights, dose_factors, *consts)
    printed = jax.nn.sigmoid(
        steepness * (dose_factors[None, :, None, None] * intensity[:, None] - threshold)
    )
    return params, printed


def solution(mesh):
    in_specs = (P("slab", "kern"), P("slab", None), P("kern", None, None, "slab"), P("kern"), P())
    out_specs = (P("slab", "kern"), P(None, None, "slab", "kern"))
    return jax.shard_map(body, mesh=mesh, in_specs=in_specs, out_specs=out_specs, check_vma=False)
```

```python
import math

import jax
import jax.numpy as jnp
import ml_dtypes
import numpy as np
from jax import lax
from jax.experimental import pallas as pl
from jax.experimental.pallas import tpu as pltpu
from jax.sharding import PartitionSpec as P

N = 2048
F = 512
STEPS = 2
HALF = N // 2
EVEN = F // 2
KERNS = 16
SLABS = 16
PEERS = 64

steepness = 3.0
threshold = 1.0
step_rate = 0.4
MESH = pl.DeviceIdType.MESH


def tables():
    scale = 1.0 / math.sqrt(N)

    def waves(index):
        phases = ((index[:, None] - F // 2) * np.arange(HALF)[None, :]) % N
        angles = phases * (2.0 * math.pi / N)
        return np.cos(angles) * scale, np.sin(angles) * scale

    cos, sin = waves(np.concatenate([np.arange(0, F, 2), np.arange(1, F, 2)]))
    y, z, k, i = np.meshgrid(np.arange(2), np.arange(2), np.arange(8), np.arange(16), indexing="ij")
    rows = [((y * 4 + 2 * h + z) * 128 + k * 16 + i).reshape(-1) for h in range(2)]
    both = np.stack([cos.reshape(2, EVEN, HALF), sin.reshape(2, EVEN, HALF)], 1).reshape(2 * F, HALF)
    to_rows = np.stack([both[:, r].T for r in rows])
    to_freq = to_rows.transpose(0, 2, 1).reshape(2, 2 * F, 32, 2, 8).transpose(0, 1, 3, 2, 4).reshape(2, 2 * F, 512)
    p, y, z, h, t = np.meshgrid(
        np.arange(2), np.arange(4), np.arange(2), np.arange(2), np.arange(16), indexing="ij"
    )
    cos, sin = waves((32 * (4 * y + 2 * h + z) + 2 * t + p).reshape(-1))
    to_cols = np.concatenate([cos, sin], 1)
    from_cols = np.concatenate([cos[:EVEN].T, sin[:EVEN].T, cos[EVEN:].T, sin[EVEN:].T], 1)
    c, s = cos.reshape(2, 8, 32, HALF), sin.reshape(2, 8, 32, HALF)
    mixed = np.stack([c, -s], 2).reshape(2, F, HALF)
    cast = lambda table: np.ascontiguousarray(table).astype(np.float32).astype(ml_dtypes.bfloat16)
    return [cast(t) for t in (mixed.transpose(0, 2, 1), to_freq, to_rows, to_cols, from_cols, mixed)]


def dot(left, right):
    return jnp.dot(left, right, preferred_element_type=jnp.float32)


def low(value):
    return value.astype(jnp.bfloat16)


def wide(value):
    return value.astype(jnp.float32)


def lane(value):
    return lax.broadcasted_iota(jnp.int32, value.shape, len(value.shape) - 1)


def is_front(value):
    return lane(value) < 64


def is_real(value):
    return lane(value) % 64 < 32


def roll(value, by):
    return pltpu.roll(value, by, 1)


def swap(value):
    return jnp.where(is_real(value), roll(value, 96), roll(value, 32))


def fronts(first, second):
    front = is_front(first)
    return jnp.where(front, first, roll(second, 64)), jnp.where(front, roll(first, 64), second)


def columns_spectrum(x, table, par):
    turned = jnp.where(is_real(x), swap(x), -swap(x))
    front = is_front(x)
    both = jnp.concatenate([jnp.where(front, x, roll(turned, 64)), jnp.where(front, roll(x, 64), turned)], 0)
    out = dot(table[par * F : par * F + F, :], low(both))
    one = jnp.where(is_front(out[:EVEN]), out[:EVEN], out[EVEN:])
    return one + roll(one, 64)


def rows_spectrum(x, table, par):
    x = jnp.concatenate([x[:, :8].reshape(256, 128), x[:, 8:].reshape(256, 128)], 0)
    turned = jnp.where(is_real(x), swap(x), -swap(x))
    at = par * F
    return dot(table[at : at + EVEN, :], low(x)) + dot(table[at + EVEN : at + F, :], low(turned))


def pixel_rows(spec, table, par):
    turned = jnp.where(is_real(spec), -swap(spec), swap(spec))
    return dot(table[:, par * F : par * F + F], low(jnp.concatenate([spec, turned], 0)))


def side_by_side(rows):
    rows = rows.reshape(32, 2, 8, 128)
    return low(jnp.where(is_front(rows[:, 0]), rows[:, 0], rows[:, 1]))


def regroup(tiles):
    a, c = fronts(tiles[0], tiles[2])
    b, d = fronts(tiles[1], tiles[3])
    out = []
    for p, q in ((a, b), (c, d)):
        real = is_real(p)
        out += [jnp.where(real, p, roll(q, 32)), jnp.where(real, roll(p, 96), q)]
    return out


def field(lefts, table, chunk):
    fields = []
    for par, left in enumerate(lefts):
        rows = slice(par * EVEN, par * EVEN + EVEN)
        with_cos = dot(left, table[rows, chunk * 256 : chunk * 256 + 256])
        with_sin = dot(left, table[rows, HALF + chunk * 256 : HALF + chunk * 256 + 256])
        fields.append((with_cos[:128] - with_sin[128:], with_cos[128:] + with_sin[:128]))
    (e_re, e_im), (o_re, o_im) = fields
    return (e_re + o_re, e_im + o_im), (e_re - o_re, e_im - o_im)


def light(e):
    power = e[0] * e[0] + e[1] * e[1]
    return jnp.sum(power.reshape(8, 16, 256), axis=0)


def sensitivity(intensity, target, doses):
    total = 0.0
    for dose in doses:
        printed = jax.nn.sigmoid(steepness * (dose * intensity - threshold))
        total = total + (printed - target) * printed * (1.0 - printed) * (steepness * dose)
    return total


def cotangent(e, sens):
    spread = jnp.broadcast_to((2.0 * sens)[None], (8, 16, 256)).reshape(128, 256)
    return jnp.concatenate([spread * e[0], spread * e[1]], 0)


def back_parts(part):
    return part[:128, :EVEN] + part[128:, EVEN:], part[128:, :EVEN] - part[:128, EVEN:]


def grad_part(got, table):
    blocks = jnp.sum(wide(got).reshape(8, 8, 8, 128), axis=1)
    tiles = [jnp.concatenate(fronts(blocks[2 * j], blocks[2 * j + 1]), 0) for j in range(4)]
    return dot(low(jnp.concatenate(tiles, 1)), table[:, :])


def kernel(mask_hbm, target_hbm, h_hbm, weight_ref, dose_ref, *rest):
    table_hbm = rest[:6]
    params_out, grad_out, light_out = rest[6:9]
    (
        t_mask, t_freq_a, t_freq_b, t_rows_a, t_rows_b, t_cols, t_back, t_mix,
        h_raw, h_re, h_im, h_turn, target, cots,
        home, s0, r0, r_par, hs, hr, s9, r9, s10, r10, s11, r11,
        s_a, r_a, s_sp, r_sp, s_b, r_b, s_db, r_db, s_d, r_d, s_da, r_da, s_g, r_g,
        local_sem, send_sem, recv_sem,
    ) = rest[9:]
    me_k, me_s = lax.axis_index("kern"), lax.axis_index("slab")
    kappa, core = me_k // 2, me_k % 2
    z0, x_at = kappa // 4, kappa % 4
    y_at, z2, z1 = me_s // 4, (me_s % 4) // 2, me_s % 2
    place = y_at * 16 + z1 * 8 + kappa
    block = 2 * y_at + z1
    sign = (1 - 2 * core).astype(jnp.float32)

    def device(x, y, z2, z1, z0, core):
        return (2 * (4 * z0 + x) + core, 4 * y + 2 * z2 + z1)

    sibling = (me_k + 1 - 2 * core, me_s)

    barrier = pltpu.get_barrier_semaphore()

    def greet(t, carry):
        slab = lax.rem(me_s + t, SLABS)
        kern = lax.rem(me_k + t, KERNS)
        pl.semaphore_signal(barrier, inc=1, device_id=(me_k, slab), device_id_type=MESH)
        pl.semaphore_signal(barrier, inc=1, device_id=(kern, me_s), device_id_type=MESH)
        return carry

    pl.semaphore_signal(
        barrier, inc=1, device_id=device(x_at, y_at, 1 - z2, z1, 1 - z0, core), device_id_type=MESH
    )
    lax.fori_loop(1, 16, greet, 0)

    own_block = pltpu.make_async_copy(mask_hbm, home, local_sem.at[8])
    load_target = pltpu.make_async_copy(
        target_hbm.at[pl.ds(pl.multiple_of(16 * kappa, 16), 16)], target, local_sem.at[9]
    )
    loads = [
        pltpu.make_async_copy(src, dst, local_sem.at[n])
        for n, (src, dst) in enumerate(
            (
                (table_hbm[0].at[core], t_mask),
                (table_hbm[1].at[core], t_freq_a),
                (table_hbm[2].at[z2], t_rows_b),
                (table_hbm[3], t_cols),
                (table_hbm[4], t_back),
                (table_hbm[1].at[z2], t_freq_b),
                (table_hbm[2].at[core], t_rows_a),
                (table_hbm[5].at[core], t_mix),
            )
        )
    ]
    own_block.start()
    for b in range(4):
        pltpu.make_async_copy(h_hbm.at[:, :, pl.ds(128 * b, 128)], h_raw.at[b], local_sem.at[10]).start()
    for load in loads:
        load.start()
    load_target.start()

    own_block.wait()
    s0[...] = low(jnp.tanh(home[...])).reshape(8, 16, 128)

    pltpu.make_async_copy(h_raw, h_raw, local_sem.at[10]).wait()
    root = jnp.sqrt(jnp.full((16, 128), weight_ref[0], jnp.float32))
    for q in range(2):
        for part in range(2):
            for b in range(4):
                own_rows = h_raw[b, part, pl.ds(q, 16, stride=2), :]
                hs[q, 16 * part : 16 * part + 16, 128 * b : 128 * b + 128] = low(own_rows * root)

    pl.semaphore_wait(barrier, 31)

    sent = []

    def send(phase, src, dst, where):
        pltpu.make_async_remote_copy(
            src_ref=src, dst_ref=dst, send_sem=send_sem.at[phase], recv_sem=recv_sem.at[phase],
            device_id=where, device_id_type=MESH,
        ).start()

    def maybe_own(phase, src, dst, where, is_own):
        if is_own is True:
            pltpu.make_async_copy(src, dst, recv_sem.at[phase]).start()
            return

        @pl.when(is_own)
        def _():
            pltpu.make_async_copy(src, dst, recv_sem.at[phase]).start()

        @pl.when(jnp.logical_not(is_own))
        def _():
            send(phase, src, dst, where)

    def sent_maybe(phase, buffer, is_own):
        @pl.when(jnp.logical_not(is_own))
        def _():
            pltpu.make_async_copy(buffer, buffer, send_sem.at[phase]).wait()

    def take(phase, buffer):
        pltpu.make_async_copy(buffer, buffer, recv_sem.at[phase]).wait()

    def given(phase, buffer):
        pltpu.make_async_copy(buffer, buffer, send_sem.at[phase]).wait()

    steps_apart = (2, 1, 3, 0)
    nested = [
        (dx, dy, da, db) for dx in steps_apart for dy in steps_apart for da, db in ((1, 1), (1, 0), (0, 1), (0, 0))
    ]

    def direct(phase, copy, dst, is_own):
        for dx, dy, da, db in nested:
            src, where = copy(lax.rem(x_at + dx, 4), lax.rem(y_at + dy, 4), da, db)
            if (dx, dy, da, db) == (0, 0, 0, 0):
                maybe_own(phase, src, dst, where, is_own)
            else:
                send(phase, src, dst, where)
        sent.append((phase, is_own))

    def exchange(phase, src, dst, step, q):
        rows = pl.ds(q * EVEN, EVEN)
        send(phase, src.at[step, rows], dst.at[step, rows], sibling)

    def flip(bit, by):
        return 1 - bit if by else bit

    def out_rows(t, carry):
        kern = lax.rem(me_k + t, KERNS)
        send(0, s0.at[kern // 2], r0.at[me_k], (kern, me_s))
        return carry

    def out_params(t, carry):
        kern = lax.rem(me_k + t, KERNS)
        send(2, home.at[pl.ds(pl.multiple_of(16 * (kern // 2), 16), 16)], r_par.at[me_k], (kern, me_s))
        return carry

    lax.fori_loop(1, KERNS, out_rows, 0, unroll=True)
    r0[me_k] = s0[kappa]

    for dq, dz in ((1, 1), (0, 1), (1, 0), (0, 0)):
        to_par = flip(z0, dq)
        where = device(x_at, y_at, flip(z2, dz), z1, to_par, core)
        if dq or dz:
            send(1, hs.at[to_par], hr.at[2 * z0 + z2], where)
        else:
            maybe_own(1, hs.at[to_par], hr.at[2 * z0 + z2], where, True)

    lax.fori_loop(1, KERNS, out_params, 0, unroll=True)
    r_par[me_k] = home[pl.ds(pl.multiple_of(16 * kappa, 16), 16), :]
    take(0, r0.at[pl.ds(0, KERNS - 1)])
    mask_lo = wide(jnp.concatenate([r0[b] for b in range(8)], 1))
    mask_hi = wide(jnp.concatenate([r0[b] for b in range(8, 16)], 1))

    at_home = me_k // 8 == core
    owner_is_reader = (z0 == core) & (z2 == core)
    for step in range(STEPS):
        base = 5 + 9 * step
        first, last = step == 0, step == STEPS - 1

        if first:
            loads[0].wait()
        columns = dot(low(mask_lo + sign * mask_hi), t_mask[...])
        for j in range(4):
            tile = columns[:, 128 * j : 128 * j + 128]
            front, back = fronts(tile[:8], tile[8:])
            s_a[step, 2 * j] = low(front)
            s_a[step, 2 * j + 1] = low(back)

        def columns_out(x, y, da, db):
            to_z1 = flip(z1, db)
            return s_a.at[step, 2 * y + to_z1], device(x, y, flip(z2, da), to_z1, core, z2)

        direct(base, columns_out, r_a.at[step, place], owner_is_reader)
        if last:
            for b in range(8):
                s10[b] = lo[:, 128 * b : 128 * b + 128]
                s10[b + 8] = hi[:, 128 * b : 128 * b + 128]
            kern = 8 * core + me_k % 8
            maybe_own(5 + 9 * STEPS, s10.at[kern], r10.at[0, kappa], (kern, me_s), at_home)

            def params_home(t, carry):
                kern = 8 * core + lax.rem(me_k + t, 8)
                send(5 + 9 * STEPS, s10.at[kern], r10.at[0, kappa], (kern, me_s))
                return carry

            lax.fori_loop(1, 8, params_home, 0, unroll=True)
        if first:
            loads[1].wait()
            take(2, r_par.at[pl.ds(0, KERNS - 1)])
            lo = jnp.concatenate([r_par[b] for b in range(8)], 1)
            hi = jnp.concatenate([r_par[b] for b in range(8, 16)], 1)
            mask_lo, mask_hi = jnp.tanh(lo), jnp.tanh(hi)
        take(base, r_a.at[step])
        early, late = wide(r_a[step, :32].reshape(256, 128)), wide(r_a[step, 32:].reshape(256, 128))
        parts = []
        for q, x in enumerate((early + late, early - late)):
            rows = slice(q * EVEN, q * EVEN + EVEN)
            parts.append(columns_spectrum(x, t_freq_a, q))
            s_sp[step, rows, :] = low(parts[q])
        send(base + 1, s_sp.at[step], r_sp.at[step], sibling)
        if first:
            take(1, hr)
            flat = jnp.concatenate(
                [hr[2 * k + h, 16 * c : 16 * c + 16, :] for k in range(2) for c in range(2) for h in range(2)], 0
            )
            h_turn[...] = wide(flat).T
            for q in range(2):
                rows = slice(q * EVEN, q * EVEN + EVEN)
                h = h_turn[pl.ds(q, EVEN, stride=2), :]
                swapped = swap(h)
                h_re[rows, :] = jnp.where(is_real(h), h, swapped)
                h_im[rows, :] = jnp.where(is_real(h), -swapped, h)
            loads[2].wait()

        halves = []
        for q in range(2):
            rows = slice(q * EVEN, q * EVEN + EVEN)
            if q == 0:
                take(base + 1, r_sp.at[step])
            spec = parts[q] + wide(r_sp[step, rows, :])
            halves.append(pixel_rows(h_re[rows, :] * spec + h_im[rows, :] * swap(spec), t_rows_b, q))
        s_b[step, :32] = low(halves[0] + halves[1]).reshape(32, 16, 128)
        s_b[step, 32:] = low(halves[0] - halves[1]).reshape(32, 16, 128)

        def rows_out(x, y, da, db):
            to_z1, to_z0 = flip(z1, da), flip(z0, db)
            return s_b.at[step, y * 16 + to_z1 * 8 + to_z0 * 4 + x], device(x, y, z2, to_z1, to_z0, core)

        direct(base + 2, rows_out, r_b.at[step, z0 * 32 + block * 4 + x_at], True)
        if first:
            loads[3].wait()
            loads[4].wait()
            load_target.wait()
        take(base + 2, r_b.at[step])

        lefts = []
        for q in range(2):
            groups = []
            for m in range(2):
                tiles = [32 * q + 16 * m + 4 * g for g in range(4)]
                groups.append(regroup([wide(r_b[step, at : at + 4]).reshape(64, 128) for at in tiles]))
            order = [jnp.concatenate([groups[0][n], groups[1][n]], 1) for n in (0, 2, 1, 3)]
            lefts.append(low(jnp.concatenate(order, 0)))
        doses = [dose_ref[d] for d in range(2)]
        for chunk in range(4):
            both = []
            for n, e in enumerate(field(lefts, t_cols, chunk)):
                intensity = light(e)
                start = n * HALF + 256 * chunk
                if last:
                    for m in range(2):
                        s9[start // 128 + m] = low(intensity[:, 128 * m : 128 * m + 128])
                sens = sensitivity(intensity, wide(target[:, start : start + 256]), doses)
                both.append(cotangent(e, sens))
            cots[0, :, 256 * chunk : 256 * chunk + 256] = low(both[0] + both[1])
            cots[1, :, 256 * chunk : 256 * chunk + 256] = low(both[0] - both[1])
        for q in range(2):
            re, im = back_parts(dot(cots[q], t_back[:, q * F : q * F + F]))
            for m in range(2):
                lanes = slice(128 * m, 128 * m + 128)
                tiles = regroup([re[:64, lanes], im[:64, lanes], re[64:, lanes], im[64:, lanes]])
                for g, tile in enumerate(tiles):
                    at = 32 * q + 16 * m + 4 * g
                    s_db[step, at : at + 4] = low(tile).reshape(4, 16, 128)

        def back_out(x, y, da, db):
            to_z1, to_z0 = flip(z1, da), flip(z0, db)
            return s_db.at[step, to_z0 * 32 + (2 * y + to_z1) * 4 + x], device(x, y, z2, to_z1, to_z0, core)

        direct(base + 3, back_out, r_db.at[step, place], True)
        if first:
            loads[5].wait()
        take(base + 3, r_db.at[step])

        early, late = wide(r_db[step, :32]), wide(r_db[step, 32:])
        parts = []
        for q, x in enumerate((early + late, early - late)):
            rows = slice(q * EVEN, q * EVEN + EVEN)
            g = rows_spectrum(x, t_freq_b, q)
            part = h_re[rows, :] * g - h_im[rows, :] * swap(g)
            parts.append(part + roll(part, 64))
            s_d[step, rows, :] = low(parts[q])
        send(base + 4, s_d.at[step], r_d.at[step], sibling)
        if first:
            loads[6].wait()
        if last:
            maybe_own(3, s9.at[me_k], r9.at[core * 8 + kappa], (me_k, me_s), True)

            def light_home(t, carry):
                kern = lax.rem(me_k + t, KERNS)
                send(3, s9.at[kern], r9.at[core * 8 + kappa], (kern, me_s))
                return carry

            lax.fori_loop(1, KERNS, light_home, 0, unroll=True)
        halves = []
        for q in range(2):
            rows = slice(q * EVEN, q * EVEN + EVEN)
            if q == 0:
                take(base + 4, r_d.at[step])
            halves.append(pixel_rows(parts[q] + wide(r_d[step, rows, :]), t_rows_a, q))
        s_da[step, :32] = side_by_side(halves[0] + halves[1])
        s_da[step, 32:] = side_by_side(halves[0] - halves[1])

        def adjoint_out(x, y, da, db):
            to_z1, to_z0 = flip(z1, da), flip(z0, db)
            return s_da.at[step, y * 16 + to_z1 * 8 + to_z0 * 4 + x], device(x, y, core, to_z1, to_z0, z0)

        direct(base + 5, adjoint_out, r_da.at[step, block * 8 + z2 * 4 + x_at], owner_is_reader)
        if first:
            loads[7].wait()
        take(base + 5, r_da.at[step])

        own = grad_part(r_da[step], t_mix)
        if last:
            break
        s_g[...] = own
        send(base + 6, s_g, r_g, sibling)
        take(base + 6, r_g)
        other = r_g[...]
        lo = lo - step_rate * (own + other) * (1.0 - mask_lo * mask_lo)
        hi = hi - step_rate * (sign * (own - other)) * (1.0 - mask_hi * mask_hi)
        mask_lo, mask_hi = jnp.tanh(lo), jnp.tanh(hi)

    for b in range(8):
        s11[b] = low(own[:, 128 * b : 128 * b + 128])

    maybe_own(4, s11.at[me_k % 8], r11.at[core * 8 + kappa], (me_k, me_s), True)

    def grad_home(t, carry):
        kern = lax.rem(me_k + t, KERNS)
        send(4, s11.at[kern % 8], r11.at[core * 8 + kappa], (kern, me_s))
        return carry

    lax.fori_loop(1, KERNS, grad_home, 0, unroll=True)
    take(3, r9)
    light_out[...] = r9[...]
    for n in range(STEPS - 1):
        take(5 + 9 * STEPS + n, r10.at[n])
    params_out[...] = r10[STEPS - 2]
    take(4, r11)
    grad_out[...] = r11[...]

    given(0, r0.at[pl.ds(0, KERNS - 1)])
    given(1, hr.at[pl.ds(0, 3)])
    given(2, r_par.at[pl.ds(0, KERNS - 1)])
    given(3, s9.at[pl.ds(0, KERNS - 1)])
    given(4, r11.at[pl.ds(0, KERNS - 1)])
    for n in range(STEPS - 1):
        given(5 + 9 * STEPS + n, r10.at[n, pl.ds(0, 7)])
        sent_maybe(5 + 9 * STEPS + n, r10.at[n, 0], at_home)
    for phase, is_own in sent:
        if is_own is True:
            given(phase, r_b.at[0, pl.ds(0, PEERS - 1)])
        else:
            given(phase, r_a.at[0, pl.ds(0, PEERS - 1)])
            sent_maybe(phase, r_a.at[0, 0], is_own)
    for step in range(STEPS):
        given(5 + 9 * step + 1, s_sp.at[step])
        given(5 + 9 * step + 4, s_d.at[step])
        if step < STEPS - 1:
            given(5 + 9 * step + 6, s_g)


def finish(params_ref, grad_ref, light_ref, dose_ref, new_ref, printed_ref):
    params = params_ref[...].reshape(128, 128)
    mask = jnp.tanh(params)
    even, odd = wide(grad_ref[:8]).reshape(128, 128), wide(grad_ref[8:]).reshape(128, 128)
    sign = jnp.where(lax.axis_index("kern") < 8, 1.0, -1.0)
    new_ref[...] = params - step_rate * (even + sign * odd) * (1.0 - mask * mask)
    for c in range(2):
        intensity = wide(light_ref[8 * c : 8 * c + 8]).reshape(128, 128)
        for d in range(2):
            printed_ref[c, d] = jax.nn.sigmoid(steepness * (dose_ref[d] * intensity - threshold))


def body(mask_params, target_bits, kernels, weights, dose_factors):
    f32, bf16 = jnp.float32, jnp.bfloat16
    consts = [jnp.asarray(t) for t in tables()]
    hbm, vmem = pl.BlockSpec(memory_space=pl.ANY), pl.BlockSpec(memory_space=pltpu.VMEM)
    smem = pl.BlockSpec(memory_space=pltpu.SMEM)
    exchange = []
    for shape, send_shape, kind in (
        ((PEERS, 8, 128), (8, 8, 128), bf16),
        ((F, 128), (F, 128), bf16),
        ((PEERS, 16, 128), (PEERS, 16, 128), bf16),
        ((PEERS, 16, 128), (PEERS, 16, 128), bf16),
        ((F, 128), (F, 128), bf16),
        ((PEERS, 8, 128), (PEERS, 8, 128), bf16),
    ):
        exchange += [pltpu.VMEM((STEPS,) + send_shape, kind), pltpu.VMEM((STEPS,) + shape, kind)]
    exchange += [pltpu.VMEM((16, HALF), f32), pltpu.VMEM((16, HALF), f32)]
    blocks = (
        jax.ShapeDtypeStruct((8, 16, 128), f32),
        jax.ShapeDtypeStruct((16, 16, 128), bf16),
        jax.ShapeDtypeStruct((16, 16, 128), bf16),
    )
    home = pl.pallas_call(
        kernel,
        out_shape=blocks,
        in_specs=[hbm, hbm, hbm, smem, smem] + [hbm] * 6,
        out_specs=(vmem, vmem, vmem),
        scratch_shapes=[
            pltpu.VMEM((HALF, F), bf16),
            pltpu.VMEM((HALF, F), bf16),
            pltpu.VMEM((HALF, F), bf16),
            pltpu.VMEM((F, HALF), bf16),
            pltpu.VMEM((F, HALF), bf16),
            pltpu.VMEM((F, N), bf16),
            pltpu.VMEM((HALF, HALF), bf16),
            pltpu.VMEM((F, HALF), bf16),
            pltpu.VMEM((4, 2, 32, 128), f32),
            pltpu.VMEM((F, 128), f32),
            pltpu.VMEM((F, 128), f32),
            pltpu.VMEM((F, 128), f32),
            pltpu.VMEM((16, N), jnp.int32),
            pltpu.VMEM((2, 256, HALF), bf16),
            pltpu.VMEM((128, 128), f32),
            pltpu.VMEM((8, 16, 128), bf16),
            pltpu.VMEM((16, 16, 128), bf16),
            pltpu.VMEM((16, 16, 128), f32),
            pltpu.VMEM((2, 32, F), bf16),
            pltpu.VMEM((4, 32, F), bf16),
            pltpu.VMEM((16, 16, 128), bf16),
            pltpu.VMEM((16, 16, 128), bf16),
            pltpu.VMEM((16, 16, 128), f32),
            pltpu.VMEM((1, 8, 16, 128), f32),
            pltpu.VMEM((8, 16, 128), bf16),
            pltpu.VMEM((16, 16, 128), bf16),
        ]
        + exchange
        + [
            pltpu.SemaphoreType.DMA((11,)),
            pltpu.SemaphoreType.DMA((24,)),
            pltpu.SemaphoreType.DMA((24,)),
        ],
        compiler_params=pltpu.CompilerParams(
            collective_id=0, has_side_effects=True, vmem_limit_bytes=62 * 1024 * 1024
        ),
    )(mask_params, target_bits, kernels[0].transpose(0, 2, 1), weights, dose_factors, *consts)
    return pl.pallas_call(
        finish,
        out_shape=(jax.ShapeDtypeStruct((128, 128), f32), jax.ShapeDtypeStruct((2, 2, 128, 128), f32)),
        in_specs=[vmem, vmem, vmem, smem],
        out_specs=(vmem, vmem),
    )(*home, dose_factors)


def solution(mesh):
    in_specs = (P("slab", "kern"), P("slab", None), P("kern", None, None, "slab"), P("kern"), P())
    out_specs = (P("slab", "kern"), P(None, None, "slab", "kern"))
    return jax.shard_map(body, mesh=mesh, in_specs=in_specs, out_specs=out_specs, check_vma=False)
```

```python
import math

import jax
import jax.numpy as jnp
import ml_dtypes
import numpy as np
from jax import lax
from jax.experimental import pallas as pl
from jax.experimental.pallas import tpu as pltpu
from jax.sharding import PartitionSpec as P

N = 2048
F = 512
STEPS = 2
HALF = N // 2
EVEN = F // 2
KERNS = 16
SLABS = 16
PEERS = 64

steepness = 3.0
threshold = 1.0
step_rate = 0.4
MESH = pl.DeviceIdType.MESH


def tables():
    scale = 1.0 / math.sqrt(N)

    def waves(index):
        phases = ((index[:, None] - F // 2) * np.arange(HALF)[None, :]) % N
        angles = phases * (2.0 * math.pi / N)
        return np.cos(angles) * scale, np.sin(angles) * scale

    cos, sin = waves(np.concatenate([np.arange(0, F, 2), np.arange(1, F, 2)]))
    y, z, k, i = np.meshgrid(np.arange(2), np.arange(2), np.arange(8), np.arange(16), indexing="ij")
    rows = [((y * 4 + 2 * h + z) * 128 + k * 16 + i).reshape(-1) for h in range(2)]
    both = np.stack([cos.reshape(2, EVEN, HALF), sin.reshape(2, EVEN, HALF)], 1).reshape(2 * F, HALF)
    to_rows = np.stack([both[:, r].T for r in rows])
    to_freq = to_rows.transpose(0, 2, 1).reshape(2, 2 * F, 32, 2, 8).transpose(0, 1, 3, 2, 4).reshape(2, 2 * F, 512)
    p, y, z, h, t = np.meshgrid(
        np.arange(2), np.arange(4), np.arange(2), np.arange(2), np.arange(16), indexing="ij"
    )
    cos, sin = waves((32 * (4 * y + 2 * h + z) + 2 * t + p).reshape(-1))
    to_cols = np.concatenate([cos, sin], 1)
    from_cols = np.concatenate([cos[:EVEN].T, sin[:EVEN].T, cos[EVEN:].T, sin[EVEN:].T], 1)
    c, s = cos.reshape(2, 8, 32, HALF), sin.reshape(2, 8, 32, HALF)
    mixed = np.stack([c, -s], 2).reshape(2, F, HALF)
    cast = lambda table: np.ascontiguousarray(table).astype(np.float32).astype(ml_dtypes.bfloat16)
    return [cast(t) for t in (mixed.transpose(0, 2, 1), to_freq, to_rows, to_cols, from_cols, mixed)]


def dot(left, right):
    return jnp.dot(left, right, preferred_element_type=jnp.float32)


def low(value):
    return value.astype(jnp.bfloat16)


def wide(value):
    return value.astype(jnp.float32)


def lane(value):
    return lax.broadcasted_iota(jnp.int32, value.shape, len(value.shape) - 1)


def is_front(value):
    return lane(value) < 64


def is_real(value):
    return lane(value) % 64 < 32


def roll(value, by):
    return pltpu.roll(value, by, 1)


def swap(value):
    return jnp.where(is_real(value), roll(value, 96), roll(value, 32))


def fronts(first, second):
    front = is_front(first)
    return jnp.where(front, first, roll(second, 64)), jnp.where(front, roll(first, 64), second)


def columns_spectrum(x, table, par):
    turned = jnp.where(is_real(x), swap(x), -swap(x))
    front = is_front(x)
    both = jnp.concatenate([jnp.where(front, x, roll(turned, 64)), jnp.where(front, roll(x, 64), turned)], 0)
    out = dot(table[par * F : par * F + F, :], low(both))
    one = jnp.where(is_front(out[:EVEN]), out[:EVEN], out[EVEN:])
    return one + roll(one, 64)


def rows_spectrum(x, table, par):
    x = jnp.concatenate([x[:, :8].reshape(256, 128), x[:, 8:].reshape(256, 128)], 0)
    turned = jnp.where(is_real(x), swap(x), -swap(x))
    at = par * F
    return dot(table[at : at + EVEN, :], low(x)) + dot(table[at + EVEN : at + F, :], low(turned))


def pixel_rows(spec, table, par):
    turned = jnp.where(is_real(spec), -swap(spec), swap(spec))
    return dot(table[:, par * F : par * F + F], low(jnp.concatenate([spec, turned], 0)))


def side_by_side(rows):
    rows = rows.reshape(32, 2, 8, 128)
    return low(jnp.where(is_front(rows[:, 0]), rows[:, 0], rows[:, 1]))


def regroup(tiles):
    a, c = fronts(tiles[0], tiles[2])
    b, d = fronts(tiles[1], tiles[3])
    out = []
    for p, q in ((a, b), (c, d)):
        real = is_real(p)
        out += [jnp.where(real, p, roll(q, 32)), jnp.where(real, roll(p, 96), q)]
    return out


def field(lefts, table, chunk):
    fields = []
    for par, left in enumerate(lefts):
        rows = slice(par * EVEN, par * EVEN + EVEN)
        with_cos = dot(left, table[rows, chunk * 256 : chunk * 256 + 256])
        with_sin = dot(left, table[rows, HALF + chunk * 256 : HALF + chunk * 256 + 256])
        fields.append((with_cos[:128] - with_sin[128:], with_cos[128:] + with_sin[:128]))
    (e_re, e_im), (o_re, o_im) = fields
    return (e_re + o_re, e_im + o_im), (e_re - o_re, e_im - o_im)


def light(e):
    power = e[0] * e[0] + e[1] * e[1]
    return jnp.sum(power.reshape(8, 16, 256), axis=0)


def sensitivity(intensity, target, doses):
    total = 0.0
    for dose in doses:
        printed = jax.nn.sigmoid(steepness * (dose * intensity - threshold))
        total = total + (printed - target) * printed * (1.0 - printed) * (steepness * dose)
    return total


def cotangent(e, sens):
    spread = jnp.broadcast_to((2.0 * sens)[None], (8, 16, 256)).reshape(128, 256)
    return jnp.concatenate([spread * e[0], spread * e[1]], 0)


def back_parts(part):
    return part[:128, :EVEN] + part[128:, EVEN:], part[128:, :EVEN] - part[:128, EVEN:]


def grad_part(got, table):
    blocks = jnp.sum(wide(got).reshape(8, 8, 8, 128), axis=1)
    tiles = [jnp.concatenate(fronts(blocks[2 * j], blocks[2 * j + 1]), 0) for j in range(4)]
    return dot(low(jnp.concatenate(tiles, 1)), table[:, :])


def kernel(mask_hbm, target_hbm, h_hbm, weight_ref, dose_ref, *rest):
    table_hbm = rest[:6]
    params_out, grad_out, light_out = rest[6:9]
    (
        t_mask, t_freq_a, t_freq_b, t_rows_a, t_rows_b, t_cols, t_back, t_mix,
        h_raw, h_re, h_im, h_turn, target, cots,
        home, s0, r0, r_par, hs, hr, s9, r9, s10, r10, s11, r11,
        s_a, r_a, s_sp, r_sp, s_b, r_b, s_db, r_db, s_d, r_d, s_da, r_da, s_g, r_g,
        local_sem, send_sem, recv_sem,
    ) = rest[9:]
    me_k, me_s = lax.axis_index("kern"), lax.axis_index("slab")
    kappa, core = me_k // 2, me_k % 2
    z0, x_at = kappa // 4, kappa % 4
    y_at, z2, z1 = me_s // 4, (me_s % 4) // 2, me_s % 2
    place = y_at * 16 + z1 * 8 + kappa
    block = 2 * y_at + z1
    sign = (1 - 2 * core).astype(jnp.float32)

    def device(x, y, z2, z1, z0, core):
        return (2 * (4 * z0 + x) + core, 4 * y + 2 * z2 + z1)

    sibling = (me_k + 1 - 2 * core, me_s)

    barrier = pltpu.get_barrier_semaphore()

    def greet(t, carry):
        kern = lax.rem(me_k + t, KERNS)
        pl.semaphore_signal(barrier, inc=1, device_id=(kern, me_s), device_id_type=MESH)
        return carry

    for dy in (2, 1, 3, 0):
        for dz in (2, 1, 3, 0):
            if dy or dz:
                slab = 4 * lax.rem(y_at + dy, 4) + lax.rem(me_s + dz, 4)
                pl.semaphore_signal(barrier, inc=1, device_id=(me_k, slab), device_id_type=MESH)
    pl.semaphore_signal(
        barrier, inc=1, device_id=device(x_at, y_at, 1 - z2, z1, 1 - z0, core), device_id_type=MESH
    )
    lax.fori_loop(1, 16, greet, 0)

    own_block = pltpu.make_async_copy(mask_hbm, home, local_sem.at[8])
    load_target = pltpu.make_async_copy(
        target_hbm.at[pl.ds(pl.multiple_of(16 * kappa, 16), 16)], target, local_sem.at[9]
    )
    loads = [
        pltpu.make_async_copy(src, dst, local_sem.at[n])
        for n, (src, dst) in enumerate(
            (
                (table_hbm[0].at[core], t_mask),
                (table_hbm[1].at[core], t_freq_a),
                (table_hbm[2].at[z2], t_rows_b),
                (table_hbm[3], t_cols),
                (table_hbm[4], t_back),
                (table_hbm[1].at[z2], t_freq_b),
                (table_hbm[2].at[core], t_rows_a),
                (table_hbm[5].at[core], t_mix),
            )
        )
    ]
    own_block.start()
    for b in range(4):
        pltpu.make_async_copy(h_hbm.at[:, :, pl.ds(128 * b, 128)], h_raw.at[b], local_sem.at[10]).start()
    for load in loads:
        load.start()
    load_target.start()

    own_block.wait()
    s0[...] = low(jnp.tanh(home[...])).reshape(8, 16, 128)

    pltpu.make_async_copy(h_raw, h_raw, local_sem.at[10]).wait()
    root = jnp.sqrt(jnp.full((16, 128), weight_ref[0], jnp.float32))
    for q in range(2):
        for part in range(2):
            for b in range(4):
                own_rows = h_raw[b, part, pl.ds(q, 16, stride=2), :]
                hs[q, 16 * part : 16 * part + 16, 128 * b : 128 * b + 128] = low(own_rows * root)

    pl.semaphore_wait(barrier, 31)

    sent = []

    def send(phase, src, dst, where):
        pltpu.make_async_remote_copy(
            src_ref=src, dst_ref=dst, send_sem=send_sem.at[phase], recv_sem=recv_sem.at[phase],
            device_id=where, device_id_type=MESH,
        ).start()

    def maybe_own(phase, src, dst, where, is_own):
        if is_own is True:
            pltpu.make_async_copy(src, dst, recv_sem.at[phase]).start()
            return

        @pl.when(is_own)
        def _():
            pltpu.make_async_copy(src, dst, recv_sem.at[phase]).start()

        @pl.when(jnp.logical_not(is_own))
        def _():
            send(phase, src, dst, where)

    def sent_maybe(phase, buffer, is_own):
        @pl.when(jnp.logical_not(is_own))
        def _():
            pltpu.make_async_copy(buffer, buffer, send_sem.at[phase]).wait()

    def take(phase, buffer):
        pltpu.make_async_copy(buffer, buffer, recv_sem.at[phase]).wait()

    def given(phase, buffer):
        pltpu.make_async_copy(buffer, buffer, send_sem.at[phase]).wait()

    steps_apart = (2, 1, 3, 0)
    nested = [
        (dx, dy, da, db) for dx in steps_apart for dy in steps_apart for da, db in ((1, 1), (1, 0), (0, 1), (0, 0))
    ]

    def direct(phase, copy, dst, is_own):
        for dx, dy, da, db in nested:
            src, where = copy(lax.rem(x_at + dx, 4), lax.rem(y_at + dy, 4), da, db)
            if (dx, dy, da, db) == (0, 0, 0, 0):
                maybe_own(phase, src, dst, where, is_own)
            else:
                send(phase, src, dst, where)
        sent.append((phase, is_own))

    def exchange(phase, src, dst, step, q):
        rows = pl.ds(q * EVEN, EVEN)
        send(phase, src.at[step, rows], dst.at[step, rows], sibling)

    def flip(bit, by):
        return 1 - bit if by else bit

    def out_rows(t, carry):
        kern = lax.rem(me_k + t, KERNS)
        send(0, s0.at[kern // 2], r0.at[me_k], (kern, me_s))
        return carry

    def out_params(t, carry):
        kern = lax.rem(me_k + t, KERNS)
        send(2, home.at[pl.ds(pl.multiple_of(16 * (kern // 2), 16), 16)], r_par.at[me_k], (kern, me_s))
        return carry

    lax.fori_loop(1, KERNS, out_rows, 0, unroll=True)
    r0[me_k] = s0[kappa]

    for dq, dz in ((1, 1), (0, 1), (1, 0), (0, 0)):
        to_par = flip(z0, dq)
        where = device(x_at, y_at, flip(z2, dz), z1, to_par, core)
        if dq or dz:
            send(1, hs.at[to_par], hr.at[2 * z0 + z2], where)
        else:
            maybe_own(1, hs.at[to_par], hr.at[2 * z0 + z2], where, True)

    r_par[me_k] = home[pl.ds(pl.multiple_of(16 * kappa, 16), 16), :]
    take(0, r0.at[pl.ds(0, KERNS - 1)])
    mask_lo = wide(jnp.concatenate([r0[b] for b in range(8)], 1))
    mask_hi = wide(jnp.concatenate([r0[b] for b in range(8, 16)], 1))

    at_home = me_k // 8 == core
    owner_is_reader = (z0 == core) & (z2 == core)
    for step in range(STEPS):
        base = 5 + 9 * step
        first, last = step == 0, step == STEPS - 1

        if first:
            loads[0].wait()
        columns = dot(low(mask_lo + sign * mask_hi), t_mask[...])
        for j in range(4):
            tile = columns[:, 128 * j : 128 * j + 128]
            front, back = fronts(tile[:8], tile[8:])
            s_a[step, 2 * j] = low(front)
            s_a[step, 2 * j + 1] = low(back)

        def columns_out(x, y, da, db):
            to_z1 = flip(z1, db)
            return s_a.at[step, 2 * y + to_z1], device(x, y, flip(z2, da), to_z1, core, z2)

        direct(base, columns_out, r_a.at[step, place], owner_is_reader)
        if first:
            lax.fori_loop(1, KERNS, out_params, 0, unroll=True)
        if last:
            for b in range(8):
                s10[b] = lo[:, 128 * b : 128 * b + 128]
                s10[b + 8] = hi[:, 128 * b : 128 * b + 128]
            kern = 8 * core + me_k % 8
            maybe_own(5 + 9 * STEPS, s10.at[kern], r10.at[0, kappa], (kern, me_s), at_home)

            def params_home(t, carry):
                kern = 8 * core + lax.rem(me_k + t, 8)
                send(5 + 9 * STEPS, s10.at[kern], r10.at[0, kappa], (kern, me_s))
                return carry

            lax.fori_loop(1, 8, params_home, 0, unroll=True)
        if first:
            loads[1].wait()
            take(2, r_par.at[pl.ds(0, KERNS - 1)])
            lo = jnp.concatenate([r_par[b] for b in range(8)], 1)
            hi = jnp.concatenate([r_par[b] for b in range(8, 16)], 1)
            mask_lo, mask_hi = jnp.tanh(lo), jnp.tanh(hi)
        take(base, r_a.at[step])
        early, late = wide(r_a[step, :32].reshape(256, 128)), wide(r_a[step, 32:].reshape(256, 128))
        parts = []
        for q, x in enumerate((early + late, early - late)):
            rows = slice(q * EVEN, q * EVEN + EVEN)
            parts.append(columns_spectrum(x, t_freq_a, q))
            s_sp[step, rows, :] = low(parts[q])
        send(base + 1, s_sp.at[step], r_sp.at[step], sibling)
        if first:
            take(1, hr)
            flat = jnp.concatenate(
                [hr[2 * k + h, 16 * c : 16 * c + 16, :] for k in range(2) for c in range(2) for h in range(2)], 0
            )
            h_turn[...] = wide(flat).T
            for q in range(2):
                rows = slice(q * EVEN, q * EVEN + EVEN)
                h = h_turn[pl.ds(q, EVEN, stride=2), :]
                swapped = swap(h)
                h_re[rows, :] = jnp.where(is_real(h), h, swapped)
                h_im[rows, :] = jnp.where(is_real(h), -swapped, h)
            loads[2].wait()

        halves = []
        for q in range(2):
            rows = slice(q * EVEN, q * EVEN + EVEN)
            if q == 0:
                take(base + 1, r_sp.at[step])
            spec = parts[q] + wide(r_sp[step, rows, :])
            halves.append(pixel_rows(h_re[rows, :] * spec + h_im[rows, :] * swap(spec), t_rows_b, q))
        s_b[step, :32] = low(halves[0] + halves[1]).reshape(32, 16, 128)
        s_b[step, 32:] = low(halves[0] - halves[1]).reshape(32, 16, 128)

        def rows_out(x, y, da, db):
            to_z1, to_z0 = flip(z1, da), flip(z0, db)
            return s_b.at[step, y * 16 + to_z1 * 8 + to_z0 * 4 + x], device(x, y, z2, to_z1, to_z0, core)

        direct(base + 2, rows_out, r_b.at[step, z0 * 32 + block * 4 + x_at], True)
        if first:
            loads[3].wait()
            loads[4].wait()
            load_target.wait()
        take(base + 2, r_b.at[step])

        lefts = []
        for q in range(2):
            groups = []
            for m in range(2):
                tiles = [32 * q + 16 * m + 4 * g for g in range(4)]
                groups.append(regroup([wide(r_b[step, at : at + 4]).reshape(64, 128) for at in tiles]))
            order = [jnp.concatenate([groups[0][n], groups[1][n]], 1) for n in (0, 2, 1, 3)]
            lefts.append(low(jnp.concatenate(order, 0)))
        doses = [dose_ref[d] for d in range(2)]
        for chunk in range(4):
            both = []
            for n, e in enumerate(field(lefts, t_cols, chunk)):
                intensity = light(e)
                start = n * HALF + 256 * chunk
                if last:
                    for m in range(2):
                        s9[start // 128 + m] = low(intensity[:, 128 * m : 128 * m + 128])
                sens = sensitivity(intensity, wide(target[:, start : start + 256]), doses)
                both.append(cotangent(e, sens))
            cots[0, :, 256 * chunk : 256 * chunk + 256] = low(both[0] + both[1])
            cots[1, :, 256 * chunk : 256 * chunk + 256] = low(both[0] - both[1])
        for q in range(2):
            re, im = back_parts(dot(cots[q], t_back[:, q * F : q * F + F]))
            for m in range(2):
                lanes = slice(128 * m, 128 * m + 128)
                tiles = regroup([re[:64, lanes], im[:64, lanes], re[64:, lanes], im[64:, lanes]])
                for g, tile in enumerate(tiles):
                    at = 32 * q + 16 * m + 4 * g
                    s_db[step, at : at + 4] = low(tile).reshape(4, 16, 128)

        def back_out(x, y, da, db):
            to_z1, to_z0 = flip(z1, da), flip(z0, db)
            return s_db.at[step, to_z0 * 32 + (2 * y + to_z1) * 4 + x], device(x, y, z2, to_z1, to_z0, core)

        direct(base + 3, back_out, r_db.at[step, place], True)
        if first:
            loads[5].wait()
        take(base + 3, r_db.at[step])

        early, late = wide(r_db[step, :32]), wide(r_db[step, 32:])
        parts = []
        for q, x in enumerate((early + late, early - late)):
            rows = slice(q * EVEN, q * EVEN + EVEN)
            g = rows_spectrum(x, t_freq_b, q)
            part = h_re[rows, :] * g - h_im[rows, :] * swap(g)
            parts.append(part + roll(part, 64))
            s_d[step, rows, :] = low(parts[q])
        send(base + 4, s_d.at[step], r_d.at[step], sibling)
        if first:
            loads[6].wait()
        if last:
            maybe_own(3, s9.at[me_k], r9.at[core * 8 + kappa], (me_k, me_s), True)

            def light_home(t, carry):
                kern = lax.rem(me_k + t, KERNS)
                send(3, s9.at[kern], r9.at[core * 8 + kappa], (kern, me_s))
                return carry

            lax.fori_loop(1, KERNS, light_home, 0, unroll=True)
        halves = []
        for q in range(2):
            rows = slice(q * EVEN, q * EVEN + EVEN)
            if q == 0:
                take(base + 4, r_d.at[step])
            halves.append(pixel_rows(parts[q] + wide(r_d[step, rows, :]), t_rows_a, q))
        s_da[step, :32] = side_by_side(halves[0] + halves[1])
        s_da[step, 32:] = side_by_side(halves[0] - halves[1])

        def adjoint_out(x, y, da, db):
            to_z1, to_z0 = flip(z1, da), flip(z0, db)
            return s_da.at[step, y * 16 + to_z1 * 8 + to_z0 * 4 + x], device(x, y, core, to_z1, to_z0, z0)

        direct(base + 5, adjoint_out, r_da.at[step, block * 8 + z2 * 4 + x_at], owner_is_reader)
        if first:
            loads[7].wait()
        take(base + 5, r_da.at[step])

        own = grad_part(r_da[step], t_mix)
        if last:
            break
        s_g[...] = own
        send(base + 6, s_g, r_g, sibling)
        take(base + 6, r_g)
        other = r_g[...]
        lo = lo - step_rate * (own + other) * (1.0 - mask_lo * mask_lo)
        hi = hi - step_rate * (sign * (own - other)) * (1.0 - mask_hi * mask_hi)
        mask_lo, mask_hi = jnp.tanh(lo), jnp.tanh(hi)

    for b in range(8):
        s11[b] = low(own[:, 128 * b : 128 * b + 128])

    maybe_own(4, s11.at[me_k % 8], r11.at[core * 8 + kappa], (me_k, me_s), True)

    def grad_home(t, carry):
        kern = lax.rem(me_k + t, KERNS)
        send(4, s11.at[kern % 8], r11.at[core * 8 + kappa], (kern, me_s))
        return carry

    lax.fori_loop(1, KERNS, grad_home, 0, unroll=True)
    take(3, r9)
    light_out[...] = r9[...]
    for n in range(STEPS - 1):
        take(5 + 9 * STEPS + n, r10.at[n])
    params_out[...] = r10[STEPS - 2]
    take(4, r11)
    grad_out[...] = r11[...]

    given(0, r0.at[pl.ds(0, KERNS - 1)])
    given(1, hr.at[pl.ds(0, 3)])
    given(2, r_par.at[pl.ds(0, KERNS - 1)])
    given(3, s9.at[pl.ds(0, KERNS - 1)])
    given(4, r11.at[pl.ds(0, KERNS - 1)])
    for n in range(STEPS - 1):
        given(5 + 9 * STEPS + n, r10.at[n, pl.ds(0, 7)])
        sent_maybe(5 + 9 * STEPS + n, r10.at[n, 0], at_home)
    for phase, is_own in sent:
        if is_own is True:
            given(phase, r_b.at[0, pl.ds(0, PEERS - 1)])
        else:
            given(phase, r_a.at[0, pl.ds(0, PEERS - 1)])
            sent_maybe(phase, r_a.at[0, 0], is_own)
    for step in range(STEPS):
        given(5 + 9 * step + 1, s_sp.at[step])
        given(5 + 9 * step + 4, s_d.at[step])
        if step < STEPS - 1:
            given(5 + 9 * step + 6, s_g)


def finish(params_ref, grad_ref, light_ref, dose_ref, new_ref, printed_ref):
    params = params_ref[...].reshape(128, 128)
    mask = jnp.tanh(params)
    even, odd = wide(grad_ref[:8]).reshape(128, 128), wide(grad_ref[8:]).reshape(128, 128)
    sign = jnp.where(lax.axis_index("kern") < 8, 1.0, -1.0)
    new_ref[...] = params - step_rate * (even + sign * odd) * (1.0 - mask * mask)
    for c in range(2):
        intensity = wide(light_ref[8 * c : 8 * c + 8]).reshape(128, 128)
        for d in range(2):
            printed_ref[c, d] = jax.nn.sigmoid(steepness * (dose_ref[d] * intensity - threshold))


def body(mask_params, target_bits, kernels, weights, dose_factors):
    f32, bf16 = jnp.float32, jnp.bfloat16
    consts = [jnp.asarray(t) for t in tables()]
    hbm, vmem = pl.BlockSpec(memory_space=pl.ANY), pl.BlockSpec(memory_space=pltpu.VMEM)
    smem = pl.BlockSpec(memory_space=pltpu.SMEM)
    exchange = []
    for shape, send_shape, kind in (
        ((PEERS, 8, 128), (8, 8, 128), bf16),
        ((F, 128), (F, 128), bf16),
        ((PEERS, 16, 128), (PEERS, 16, 128), bf16),
        ((PEERS, 16, 128), (PEERS, 16, 128), bf16),
        ((F, 128), (F, 128), bf16),
        ((PEERS, 8, 128), (PEERS, 8, 128), bf16),
    ):
        exchange += [pltpu.VMEM((STEPS,) + send_shape, kind), pltpu.VMEM((STEPS,) + shape, kind)]
    exchange += [pltpu.VMEM((16, HALF), f32), pltpu.VMEM((16, HALF), f32)]
    blocks = (
        jax.ShapeDtypeStruct((8, 16, 128), f32),
        jax.ShapeDtypeStruct((16, 16, 128), bf16),
        jax.ShapeDtypeStruct((16, 16, 128), bf16),
    )
    home = pl.pallas_call(
        kernel,
        out_shape=blocks,
        in_specs=[hbm, hbm, hbm, smem, smem] + [hbm] * 6,
        out_specs=(vmem, vmem, vmem),
        scratch_shapes=[
            pltpu.VMEM((HALF, F), bf16),
            pltpu.VMEM((HALF, F), bf16),
            pltpu.VMEM((HALF, F), bf16),
            pltpu.VMEM((F, HALF), bf16),
            pltpu.VMEM((F, HALF), bf16),
            pltpu.VMEM((F, N), bf16),
            pltpu.VMEM((HALF, HALF), bf16),
            pltpu.VMEM((F, HALF), bf16),
            pltpu.VMEM((4, 2, 32, 128), f32),
            pltpu.VMEM((F, 128), f32),
            pltpu.VMEM((F, 128), f32),
            pltpu.VMEM((F, 128), f32),
            pltpu.VMEM((16, N), jnp.int32),
            pltpu.VMEM((2, 256, HALF), bf16),
            pltpu.VMEM((128, 128), f32),
            pltpu.VMEM((8, 16, 128), bf16),
            pltpu.VMEM((16, 16, 128), bf16),
            pltpu.VMEM((16, 16, 128), f32),
            pltpu.VMEM((2, 32, F), bf16),
            pltpu.VMEM((4, 32, F), bf16),
            pltpu.VMEM((16, 16, 128), bf16),
            pltpu.VMEM((16, 16, 128), bf16),
            pltpu.VMEM((16, 16, 128), f32),
            pltpu.VMEM((1, 8, 16, 128), f32),
            pltpu.VMEM((8, 16, 128), bf16),
            pltpu.VMEM((16, 16, 128), bf16),
        ]
        + exchange
        + [
            pltpu.SemaphoreType.DMA((11,)),
            pltpu.SemaphoreType.DMA((24,)),
            pltpu.SemaphoreType.DMA((24,)),
        ],
        compiler_params=pltpu.CompilerParams(
            collective_id=0, has_side_effects=True, vmem_limit_bytes=62 * 1024 * 1024
        ),
    )(mask_params, target_bits, kernels[0].transpose(0, 2, 1), weights, dose_factors, *consts)
    return pl.pallas_call(
        finish,
        out_shape=(jax.ShapeDtypeStruct((128, 128), f32), jax.ShapeDtypeStruct((2, 2, 128, 128), f32)),
        in_specs=[vmem, vmem, vmem, smem],
        out_specs=(vmem, vmem),
    )(*home, dose_factors)


def solution(mesh):
    in_specs = (P("slab", "kern"), P("slab", None), P("kern", None, None, "slab"), P("kern"), P())
    out_specs = (P("slab", "kern"), P(None, None, "slab", "kern"))
    return jax.shard_map(body, mesh=mesh, in_specs=in_specs, out_specs=out_specs, check_vma=False)
```

```python
import math

import jax
import jax.numpy as jnp
import ml_dtypes
import numpy as np
from jax import lax
from jax.experimental import pallas as pl
from jax.experimental.pallas import tpu as pltpu
from jax.sharding import PartitionSpec as P

N = 2048
F = 512
STEPS = 2
HALF = N // 2
EVEN = F // 2
KERNS = 16
SLABS = 16
PEERS = 64

steepness = 3.0
threshold = 1.0
step_rate = 0.4
MESH = pl.DeviceIdType.MESH


def tables():
    scale = 1.0 / math.sqrt(N)

    def waves(index):
        phases = ((index[:, None] - F // 2) * np.arange(HALF)[None, :]) % N
        angles = phases * (2.0 * math.pi / N)
        return np.cos(angles) * scale, np.sin(angles) * scale

    cos, sin = waves(np.concatenate([np.arange(0, F, 2), np.arange(1, F, 2)]))
    y, z, k, i = np.meshgrid(np.arange(2), np.arange(2), np.arange(8), np.arange(16), indexing="ij")
    rows = [((y * 4 + 2 * h + z) * 128 + k * 16 + i).reshape(-1) for h in range(2)]
    both = np.stack([cos.reshape(2, EVEN, HALF), sin.reshape(2, EVEN, HALF)], 1).reshape(2 * F, HALF)
    to_rows = np.stack([both[:, r].T for r in rows])
    to_freq = to_rows.transpose(0, 2, 1).reshape(2, 2 * F, 32, 2, 8).transpose(0, 1, 3, 2, 4).reshape(2, 2 * F, 512)
    p, y, z, h, t = np.meshgrid(
        np.arange(2), np.arange(4), np.arange(2), np.arange(2), np.arange(16), indexing="ij"
    )
    cos, sin = waves((32 * (4 * y + 2 * h + z) + 2 * t + p).reshape(-1))
    to_cols = np.concatenate([cos, sin], 1)
    from_cols = np.concatenate([cos[:EVEN].T, sin[:EVEN].T, cos[EVEN:].T, sin[EVEN:].T], 1)
    c, s = cos.reshape(2, 8, 32, HALF), sin.reshape(2, 8, 32, HALF)
    mixed = np.stack([c, -s], 2).reshape(2, F, HALF)
    cast = lambda table: np.ascontiguousarray(table).astype(np.float32).astype(ml_dtypes.bfloat16)
    return [cast(t) for t in (mixed.transpose(0, 2, 1), to_freq, to_rows, to_cols, from_cols, mixed)]


def dot(left, right):
    return jnp.dot(left, right, preferred_element_type=jnp.float32)


def low(value):
    return value.astype(jnp.bfloat16)


def wide(value):
    return value.astype(jnp.float32)


def lane(value):
    return lax.broadcasted_iota(jnp.int32, value.shape, len(value.shape) - 1)


def is_front(value):
    return lane(value) < 64


def is_real(value):
    return lane(value) % 64 < 32


def roll(value, by):
    return pltpu.roll(value, by, 1)


def swap(value):
    return jnp.where(is_real(value), roll(value, 96), roll(value, 32))


def fronts(first, second):
    front = is_front(first)
    return jnp.where(front, first, roll(second, 64)), jnp.where(front, roll(first, 64), second)


def columns_spectrum(x, table, par):
    turned = jnp.where(is_real(x), swap(x), -swap(x))
    front = is_front(x)
    both = jnp.concatenate([jnp.where(front, x, roll(turned, 64)), jnp.where(front, roll(x, 64), turned)], 0)
    out = dot(table[par * F : par * F + F, :], low(both))
    one = jnp.where(is_front(out[:EVEN]), out[:EVEN], out[EVEN:])
    return one + roll(one, 64)


def rows_spectrum(x, table, par):
    x = jnp.concatenate([x[:, :8].reshape(256, 128), x[:, 8:].reshape(256, 128)], 0)
    turned = jnp.where(is_real(x), swap(x), -swap(x))
    at = par * F
    return dot(table[at : at + EVEN, :], low(x)) + dot(table[at + EVEN : at + F, :], low(turned))


def pixel_rows(spec, table, par):
    turned = jnp.where(is_real(spec), -swap(spec), swap(spec))
    return dot(table[:, par * F : par * F + F], low(jnp.concatenate([spec, turned], 0)))


def side_by_side(rows):
    rows = rows.reshape(32, 2, 8, 128)
    return low(jnp.where(is_front(rows[:, 0]), rows[:, 0], rows[:, 1]))


def regroup(tiles):
    a, c = fronts(tiles[0], tiles[2])
    b, d = fronts(tiles[1], tiles[3])
    out = []
    for p, q in ((a, b), (c, d)):
        real = is_real(p)
        out += [jnp.where(real, p, roll(q, 32)), jnp.where(real, roll(p, 96), q)]
    return out


def field(lefts, table, chunk):
    fields = []
    for par, left in enumerate(lefts):
        rows = slice(par * EVEN, par * EVEN + EVEN)
        with_cos = dot(left, table[rows, chunk * 256 : chunk * 256 + 256])
        with_sin = dot(left, table[rows, HALF + chunk * 256 : HALF + chunk * 256 + 256])
        fields.append((with_cos[:128] - with_sin[128:], with_cos[128:] + with_sin[:128]))
    (e_re, e_im), (o_re, o_im) = fields
    return (e_re + o_re, e_im + o_im), (e_re - o_re, e_im - o_im)


def light(e):
    power = e[0] * e[0] + e[1] * e[1]
    return jnp.sum(power.reshape(8, 16, 256), axis=0)


def sensitivity(intensity, target, doses):
    total = 0.0
    for dose in doses:
        printed = jax.nn.sigmoid(steepness * (dose * intensity - threshold))
        total = total + (printed - target) * printed * (1.0 - printed) * (steepness * dose)
    return total


def cotangent(e, sens):
    spread = jnp.broadcast_to((2.0 * sens)[None], (8, 16, 256)).reshape(128, 256)
    return jnp.concatenate([spread * e[0], spread * e[1]], 0)


def back_parts(part):
    return part[:128, :EVEN] + part[128:, EVEN:], part[128:, :EVEN] - part[:128, EVEN:]


def grad_part(got, table):
    blocks = jnp.sum(wide(got).reshape(8, 8, 8, 128), axis=1)
    tiles = [jnp.concatenate(fronts(blocks[2 * j], blocks[2 * j + 1]), 0) for j in range(4)]
    return dot(low(jnp.concatenate(tiles, 1)), table[:, :])


def kernel(mask_hbm, target_hbm, h_hbm, weight_ref, dose_ref, *rest):
    table_hbm = rest[:6]
    params_out, grad_out, light_out = rest[6:9]
    (
        t_mask, t_freq_a, t_freq_b, t_rows_a, t_rows_b, t_cols, t_back, t_mix,
        h_raw, h_re, h_im, h_turn, target, cots,
        home, s0, r0, r_par, hs, hr, s9, r9, s10, r10, s11, r11,
        s_a, r_a, s_sp, r_sp, s_b, r_b, s_db, r_db, s_d, r_d, s_da, r_da, s_g, r_g,
        local_sem, send_sem, recv_sem,
    ) = rest[9:]
    me_k, me_s = lax.axis_index("kern"), lax.axis_index("slab")
    kappa, core = me_k // 2, me_k % 2
    z0, x_at = kappa // 4, kappa % 4
    y_at, z2, z1 = me_s // 4, (me_s % 4) // 2, me_s % 2
    place = y_at * 16 + z1 * 8 + kappa
    block = 2 * y_at + z1
    sign = (1 - 2 * core).astype(jnp.float32)

    def device(x, y, z2, z1, z0, core):
        return (2 * (4 * z0 + x) + core, 4 * y + 2 * z2 + z1)

    sibling = (me_k + 1 - 2 * core, me_s)

    barrier = pltpu.get_barrier_semaphore()

    def greet(t, carry):
        kern = lax.rem(me_k + t, KERNS)
        pl.semaphore_signal(barrier, inc=1, device_id=(kern, me_s), device_id_type=MESH)
        return carry

    for dy in (2, 1, 3, 0):
        for dz in (2, 1, 3, 0):
            if dy or dz:
                slab = 4 * lax.rem(y_at + dy, 4) + lax.rem(me_s + dz, 4)
                pl.semaphore_signal(barrier, inc=1, device_id=(me_k, slab), device_id_type=MESH)
    pl.semaphore_signal(
        barrier, inc=1, device_id=device(x_at, y_at, 1 - z2, z1, 1 - z0, core), device_id_type=MESH
    )
    lax.fori_loop(1, 16, greet, 0)

    own_block = pltpu.make_async_copy(mask_hbm, home, local_sem.at[8])
    load_target = pltpu.make_async_copy(
        target_hbm.at[pl.ds(pl.multiple_of(16 * kappa, 16), 16)], target, local_sem.at[9]
    )
    loads = [
        pltpu.make_async_copy(src, dst, local_sem.at[n])
        for n, (src, dst) in enumerate(
            (
                (table_hbm[0].at[core], t_mask),
                (table_hbm[1].at[core], t_freq_a),
                (table_hbm[2].at[z2], t_rows_b),
                (table_hbm[3], t_cols),
                (table_hbm[4], t_back),
                (table_hbm[1].at[z2], t_freq_b),
                (table_hbm[2].at[core], t_rows_a),
                (table_hbm[5].at[core], t_mix),
            )
        )
    ]
    own_block.start()
    for b in range(4):
        pltpu.make_async_copy(h_hbm.at[:, :, pl.ds(128 * b, 128)], h_raw.at[b], local_sem.at[10]).start()
    for load in loads:
        load.start()
    load_target.start()

    own_block.wait()
    s0[...] = low(jnp.tanh(home[...])).reshape(8, 16, 128)

    pltpu.make_async_copy(h_raw, h_raw, local_sem.at[10]).wait()
    root = jnp.sqrt(jnp.full((16, 128), weight_ref[0], jnp.float32))
    for q in range(2):
        for part in range(2):
            for b in range(4):
                own_rows = h_raw[b, part, pl.ds(q, 16, stride=2), :]
                hs[q, 16 * part : 16 * part + 16, 128 * b : 128 * b + 128] = low(own_rows * root)

    pl.semaphore_wait(barrier, 31)

    sent = []

    def send(phase, src, dst, where):
        pltpu.make_async_remote_copy(
            src_ref=src, dst_ref=dst, send_sem=send_sem.at[phase], recv_sem=recv_sem.at[phase],
            device_id=where, device_id_type=MESH,
        ).start()

    def maybe_own(phase, src, dst, where, is_own):
        if is_own is True:
            pltpu.make_async_copy(src, dst, recv_sem.at[phase]).start()
            return

        @pl.when(is_own)
        def _():
            pltpu.make_async_copy(src, dst, recv_sem.at[phase]).start()

        @pl.when(jnp.logical_not(is_own))
        def _():
            send(phase, src, dst, where)

    def sent_maybe(phase, buffer, is_own):
        @pl.when(jnp.logical_not(is_own))
        def _():
            pltpu.make_async_copy(buffer, buffer, send_sem.at[phase]).wait()

    def take(phase, buffer):
        pltpu.make_async_copy(buffer, buffer, recv_sem.at[phase]).wait()

    def given(phase, buffer):
        pltpu.make_async_copy(buffer, buffer, send_sem.at[phase]).wait()

    steps_apart = (2, 1, 3, 0)
    nested = [
        (dx, dy, da, db) for dx in steps_apart for dy in steps_apart for da, db in ((1, 1), (1, 0), (0, 1), (0, 0))
    ]

    def direct(phase, copy, dst, is_own):
        for dx, dy, da, db in nested:
            src, where = copy(lax.rem(x_at + dx, 4), lax.rem(y_at + dy, 4), da, db)
            if (dx, dy, da, db) == (0, 0, 0, 0):
                maybe_own(phase, src, dst, where, is_own)
            else:
                send(phase, src, dst, where)
        sent.append((phase, is_own))

    def exchange(phase, src, dst, step, q):
        rows = pl.ds(q * EVEN, EVEN)
        send(phase, src.at[step, rows], dst.at[step, rows], sibling)

    def flip(bit, by):
        return 1 - bit if by else bit

    def out_rows(t, carry):
        kern = lax.rem(me_k + t, KERNS)
        send(0, s0.at[kern // 2], r0.at[me_k], (kern, me_s))
        return carry

    def out_params(t, carry):
        kern = lax.rem(me_k + t, KERNS)
        send(2, home.at[pl.ds(pl.multiple_of(16 * (kern // 2), 16), 16)], r_par.at[me_k], (kern, me_s))
        return carry

    lax.fori_loop(1, KERNS, out_rows, 0, unroll=True)
    r0[me_k] = s0[kappa]

    for dq, dz in ((1, 1), (0, 1), (1, 0), (0, 0)):
        to_par = flip(z0, dq)
        where = device(x_at, y_at, flip(z2, dz), z1, to_par, core)
        if dq or dz:
            send(1, hs.at[to_par], hr.at[2 * z0 + z2], where)
        else:
            maybe_own(1, hs.at[to_par], hr.at[2 * z0 + z2], where, True)

    r_par[me_k] = home[pl.ds(pl.multiple_of(16 * kappa, 16), 16), :]
    take(0, r0.at[pl.ds(0, KERNS - 1)])
    mask_lo = wide(jnp.concatenate([r0[b] for b in range(8)], 1))
    mask_hi = wide(jnp.concatenate([r0[b] for b in range(8, 16)], 1))

    at_home = me_k // 8 == core
    owner_is_reader = (z0 == core) & (z2 == core)
    for step in range(STEPS):
        base = 5 + 9 * step
        first, last = step == 0, step == STEPS - 1

        if first:
            loads[0].wait()
        columns = dot(low(mask_lo + sign * mask_hi), t_mask[...])
        for j in range(4):
            tile = columns[:, 128 * j : 128 * j + 128]
            front, back = fronts(tile[:8], tile[8:])
            s_a[step, 2 * j] = low(front)
            s_a[step, 2 * j + 1] = low(back)

        def columns_out(x, y, da, db):
            to_z1 = flip(z1, db)
            return s_a.at[step, 2 * y + to_z1], device(x, y, flip(z2, da), to_z1, core, z2)

        direct(base, columns_out, r_a.at[step, place], owner_is_reader)
        if last:
            for b in range(8):
                s10[b] = lo[:, 128 * b : 128 * b + 128]
                s10[b + 8] = hi[:, 128 * b : 128 * b + 128]
            kern = 8 * core + me_k % 8
            maybe_own(5 + 9 * STEPS, s10.at[kern], r10.at[0, kappa], (kern, me_s), at_home)

            def params_home(t, carry):
                kern = 8 * core + lax.rem(me_k + t, 8)
                send(5 + 9 * STEPS, s10.at[kern], r10.at[0, kappa], (kern, me_s))
                return carry

            lax.fori_loop(1, 8, params_home, 0, unroll=True)
        if first:
            take(1, hr)
            flat = jnp.concatenate(
                [hr[2 * k + h, 16 * c : 16 * c + 16, :] for k in range(2) for c in range(2) for h in range(2)], 0
            )
            h_turn[...] = wide(flat).T
            for q in range(2):
                rows = slice(q * EVEN, q * EVEN + EVEN)
                h = h_turn[pl.ds(q, EVEN, stride=2), :]
                swapped = swap(h)
                h_re[rows, :] = jnp.where(is_real(h), h, swapped)
                h_im[rows, :] = jnp.where(is_real(h), -swapped, h)
            loads[2].wait()
            loads[1].wait()
        take(base, r_a.at[step])
        early, late = wide(r_a[step, :32].reshape(256, 128)), wide(r_a[step, 32:].reshape(256, 128))
        parts = []
        for q, x in enumerate((early + late, early - late)):
            rows = slice(q * EVEN, q * EVEN + EVEN)
            parts.append(columns_spectrum(x, t_freq_a, q))
            s_sp[step, rows, :] = low(parts[q])
        send(base + 1, s_sp.at[step], r_sp.at[step], sibling)

        halves = []
        for q in range(2):
            rows = slice(q * EVEN, q * EVEN + EVEN)
            if q == 0:
                take(base + 1, r_sp.at[step])
            spec = parts[q] + wide(r_sp[step, rows, :])
            halves.append(pixel_rows(h_re[rows, :] * spec + h_im[rows, :] * swap(spec), t_rows_b, q))
        s_b[step, :32] = low(halves[0] + halves[1]).reshape(32, 16, 128)
        s_b[step, 32:] = low(halves[0] - halves[1]).reshape(32, 16, 128)

        def rows_out(x, y, da, db):
            to_z1, to_z0 = flip(z1, da), flip(z0, db)
            return s_b.at[step, y * 16 + to_z1 * 8 + to_z0 * 4 + x], device(x, y, z2, to_z1, to_z0, core)

        direct(base + 2, rows_out, r_b.at[step, z0 * 32 + block * 4 + x_at], True)
        if first:
            loads[3].wait()
            loads[4].wait()
            load_target.wait()
        take(base + 2, r_b.at[step])

        lefts = []
        for q in range(2):
            groups = []
            for m in range(2):
                tiles = [32 * q + 16 * m + 4 * g for g in range(4)]
                groups.append(regroup([wide(r_b[step, at : at + 4]).reshape(64, 128) for at in tiles]))
            order = [jnp.concatenate([groups[0][n], groups[1][n]], 1) for n in (0, 2, 1, 3)]
            lefts.append(low(jnp.concatenate(order, 0)))
        doses = [dose_ref[d] for d in range(2)]
        for chunk in range(4):
            both = []
            for n, e in enumerate(field(lefts, t_cols, chunk)):
                intensity = light(e)
                start = n * HALF + 256 * chunk
                if last:
                    for m in range(2):
                        s9[start // 128 + m] = low(intensity[:, 128 * m : 128 * m + 128])
                sens = sensitivity(intensity, wide(target[:, start : start + 256]), doses)
                both.append(cotangent(e, sens))
            cots[0, :, 256 * chunk : 256 * chunk + 256] = low(both[0] + both[1])
            cots[1, :, 256 * chunk : 256 * chunk + 256] = low(both[0] - both[1])
        for q in range(2):
            re, im = back_parts(dot(cots[q], t_back[:, q * F : q * F + F]))
            for m in range(2):
                lanes = slice(128 * m, 128 * m + 128)
                tiles = regroup([re[:64, lanes], im[:64, lanes], re[64:, lanes], im[64:, lanes]])
                for g, tile in enumerate(tiles):
                    at = 32 * q + 16 * m + 4 * g
                    s_db[step, at : at + 4] = low(tile).reshape(4, 16, 128)

        def back_out(x, y, da, db):
            to_z1, to_z0 = flip(z1, da), flip(z0, db)
            return s_db.at[step, to_z0 * 32 + (2 * y + to_z1) * 4 + x], device(x, y, z2, to_z1, to_z0, core)

        direct(base + 3, back_out, r_db.at[step, place], True)
        if first:
            lax.fori_loop(1, KERNS, out_params, 0, unroll=True)
            loads[5].wait()
        take(base + 3, r_db.at[step])

        early, late = wide(r_db[step, :32]), wide(r_db[step, 32:])
        parts = []
        for q, x in enumerate((early + late, early - late)):
            rows = slice(q * EVEN, q * EVEN + EVEN)
            g = rows_spectrum(x, t_freq_b, q)
            part = h_re[rows, :] * g - h_im[rows, :] * swap(g)
            parts.append(part + roll(part, 64))
            s_d[step, rows, :] = low(parts[q])
        send(base + 4, s_d.at[step], r_d.at[step], sibling)
        if first:
            loads[6].wait()
        if last:
            maybe_own(3, s9.at[me_k], r9.at[core * 8 + kappa], (me_k, me_s), True)

            def light_home(t, carry):
                kern = lax.rem(me_k + t, KERNS)
                send(3, s9.at[kern], r9.at[core * 8 + kappa], (kern, me_s))
                return carry

            lax.fori_loop(1, KERNS, light_home, 0, unroll=True)
        halves = []
        for q in range(2):
            rows = slice(q * EVEN, q * EVEN + EVEN)
            if q == 0:
                take(base + 4, r_d.at[step])
            halves.append(pixel_rows(parts[q] + wide(r_d[step, rows, :]), t_rows_a, q))
        s_da[step, :32] = side_by_side(halves[0] + halves[1])
        s_da[step, 32:] = side_by_side(halves[0] - halves[1])

        def adjoint_out(x, y, da, db):
            to_z1, to_z0 = flip(z1, da), flip(z0, db)
            return s_da.at[step, y * 16 + to_z1 * 8 + to_z0 * 4 + x], device(x, y, core, to_z1, to_z0, z0)

        direct(base + 5, adjoint_out, r_da.at[step, block * 8 + z2 * 4 + x_at], owner_is_reader)
        if first:
            loads[7].wait()
            take(2, r_par.at[pl.ds(0, KERNS - 1)])
            lo = jnp.concatenate([r_par[b] for b in range(8)], 1)
            hi = jnp.concatenate([r_par[b] for b in range(8, 16)], 1)
            mask_lo, mask_hi = jnp.tanh(lo), jnp.tanh(hi)
        take(base + 5, r_da.at[step])

        own = grad_part(r_da[step], t_mix)
        if last:
            break
        s_g[...] = own
        send(base + 6, s_g, r_g, sibling)
        take(base + 6, r_g)
        other = r_g[...]
        lo = lo - step_rate * (own + other) * (1.0 - mask_lo * mask_lo)
        hi = hi - step_rate * (sign * (own - other)) * (1.0 - mask_hi * mask_hi)
        mask_lo, mask_hi = jnp.tanh(lo), jnp.tanh(hi)

    for b in range(8):
        s11[b] = low(own[:, 128 * b : 128 * b + 128])

    maybe_own(4, s11.at[me_k % 8], r11.at[core * 8 + kappa], (me_k, me_s), True)

    def grad_home(t, carry):
        kern = lax.rem(me_k + t, KERNS)
        send(4, s11.at[kern % 8], r11.at[core * 8 + kappa], (kern, me_s))
        return carry

    lax.fori_loop(1, KERNS, grad_home, 0, unroll=True)
    take(3, r9)
    light_out[...] = r9[...]
    for n in range(STEPS - 1):
        take(5 + 9 * STEPS + n, r10.at[n])
    params_out[...] = r10[STEPS - 2]
    take(4, r11)
    grad_out[...] = r11[...]

    given(0, r0.at[pl.ds(0, KERNS - 1)])
    given(1, hr.at[pl.ds(0, 3)])
    given(2, r_par.at[pl.ds(0, KERNS - 1)])
    given(3, s9.at[pl.ds(0, KERNS - 1)])
    given(4, r11.at[pl.ds(0, KERNS - 1)])
    for n in range(STEPS - 1):
        given(5 + 9 * STEPS + n, r10.at[n, pl.ds(0, 7)])
        sent_maybe(5 + 9 * STEPS + n, r10.at[n, 0], at_home)
    for phase, is_own in sent:
        if is_own is True:
            given(phase, r_b.at[0, pl.ds(0, PEERS - 1)])
        else:
            given(phase, r_a.at[0, pl.ds(0, PEERS - 1)])
            sent_maybe(phase, r_a.at[0, 0], is_own)
    for step in range(STEPS):
        given(5 + 9 * step + 1, s_sp.at[step])
        given(5 + 9 * step + 4, s_d.at[step])
        if step < STEPS - 1:
            given(5 + 9 * step + 6, s_g)


def finish(params_ref, grad_ref, light_ref, dose_ref, new_ref, printed_ref):
    params = params_ref[...].reshape(128, 128)
    mask = jnp.tanh(params)
    even, odd = wide(grad_ref[:8]).reshape(128, 128), wide(grad_ref[8:]).reshape(128, 128)
    sign = jnp.where(lax.axis_index("kern") < 8, 1.0, -1.0)
    new_ref[...] = params - step_rate * (even + sign * odd) * (1.0 - mask * mask)
    for c in range(2):
        intensity = wide(light_ref[8 * c : 8 * c + 8]).reshape(128, 128)
        for d in range(2):
            printed_ref[c, d] = jax.nn.sigmoid(steepness * (dose_ref[d] * intensity - threshold))


def body(mask_params, target_bits, kernels, weights, dose_factors):
    f32, bf16 = jnp.float32, jnp.bfloat16
    consts = [jnp.asarray(t) for t in tables()]
    hbm, vmem = pl.BlockSpec(memory_space=pl.ANY), pl.BlockSpec(memory_space=pltpu.VMEM)
    smem = pl.BlockSpec(memory_space=pltpu.SMEM)
    exchange = []
    for shape, send_shape, kind in (
        ((PEERS, 8, 128), (8, 8, 128), bf16),
        ((F, 128), (F, 128), bf16),
        ((PEERS, 16, 128), (PEERS, 16, 128), bf16),
        ((PEERS, 16, 128), (PEERS, 16, 128), bf16),
        ((F, 128), (F, 128), bf16),
        ((PEERS, 8, 128), (PEERS, 8, 128), bf16),
    ):
        exchange += [pltpu.VMEM((STEPS,) + send_shape, kind), pltpu.VMEM((STEPS,) + shape, kind)]
    exchange += [pltpu.VMEM((16, HALF), f32), pltpu.VMEM((16, HALF), f32)]
    blocks = (
        jax.ShapeDtypeStruct((8, 16, 128), f32),
        jax.ShapeDtypeStruct((16, 16, 128), bf16),
        jax.ShapeDtypeStruct((16, 16, 128), bf16),
    )
    home = pl.pallas_call(
        kernel,
        out_shape=blocks,
        in_specs=[hbm, hbm, hbm, smem, smem] + [hbm] * 6,
        out_specs=(vmem, vmem, vmem),
        scratch_shapes=[
            pltpu.VMEM((HALF, F), bf16),
            pltpu.VMEM((HALF, F), bf16),
            pltpu.VMEM((HALF, F), bf16),
            pltpu.VMEM((F, HALF), bf16),
            pltpu.VMEM((F, HALF), bf16),
            pltpu.VMEM((F, N), bf16),
            pltpu.VMEM((HALF, HALF), bf16),
            pltpu.VMEM((F, HALF), bf16),
            pltpu.VMEM((4, 2, 32, 128), f32),
            pltpu.VMEM((F, 128), f32),
            pltpu.VMEM((F, 128), f32),
            pltpu.VMEM((F, 128), f32),
            pltpu.VMEM((16, N), jnp.int32),
            pltpu.VMEM((2, 256, HALF), bf16),
            pltpu.VMEM((128, 128), f32),
            pltpu.VMEM((8, 16, 128), bf16),
            pltpu.VMEM((16, 16, 128), bf16),
            pltpu.VMEM((16, 16, 128), f32),
            pltpu.VMEM((2, 32, F), bf16),
            pltpu.VMEM((4, 32, F), bf16),
            pltpu.VMEM((16, 16, 128), bf16),
            pltpu.VMEM((16, 16, 128), bf16),
            pltpu.VMEM((16, 16, 128), f32),
            pltpu.VMEM((1, 8, 16, 128), f32),
            pltpu.VMEM((8, 16, 128), bf16),
            pltpu.VMEM((16, 16, 128), bf16),
        ]
        + exchange
        + [
            pltpu.SemaphoreType.DMA((11,)),
            pltpu.SemaphoreType.DMA((24,)),
            pltpu.SemaphoreType.DMA((24,)),
        ],
        compiler_params=pltpu.CompilerParams(
            collective_id=0, has_side_effects=True, vmem_limit_bytes=62 * 1024 * 1024
        ),
    )(mask_params, target_bits, kernels[0].transpose(0, 2, 1), weights, dose_factors, *consts)
    return pl.pallas_call(
        finish,
        out_shape=(jax.ShapeDtypeStruct((128, 128), f32), jax.ShapeDtypeStruct((2, 2, 128, 128), f32)),
        in_specs=[vmem, vmem, vmem, smem],
        out_specs=(vmem, vmem),
    )(*home, dose_factors)


def solution(mesh):
    in_specs = (P("slab", "kern"), P("slab", None), P("kern", None, None, "slab"), P("kern"), P())
    out_specs = (P("slab", "kern"), P(None, None, "slab", "kern"))
    return jax.shard_map(body, mesh=mesh, in_specs=in_specs, out_specs=out_specs, check_vma=False)
```
